128 devices in a mesh: lat: 16 (over z, x), lon: 8 (over y, core).
Axes of the slice: x: 4, y: 4, z: 4, core: 2. Of those that a mesh axis runs over, the one named last changes fastest.
Arguments:
- conductivity: bfloat16 [2, 64, 131072], P(None, None, ('lat', 'lon')), may hold values from 0.19921875 to 2
- wind_terms: bfloat16 [4, 64, 131072], P(None, None, ('lat', 'lon')), may hold values from -6 to 6
- correlation_tiles: bfloat16 [1024, 1024, 1024], P(('lat', 'lon')), may hold values from -0.1875 to 0.1875
- tile_targets: int32 [128, 8], P(('lat', 'lon')), may hold values from 0 to 15, as said below
- level_weights: float32 [64], replicated, may hold values from 0.02 to 0.2
- line_levels: int32 [2, 128, 1024], P(None, 'lat', 'lon'), may hold values from 0 to 64, as said below
- potential: float32 [128, 1024], P('lat', 'lon'), may hold values from -6 to 6
Outputs:
- stencil: float32 [9, 128, 1024], P(None, 'lat', 'lon')
- source_term: float32 [128, 1024], P('lat', 'lon')
- geo_field: float32 [2, 131072], P(None, ('lat', 'lon'))
The draws below stay inside these ranges and needn't reach their ends.
Inputs may be any that keep to these rules, and one draw needn't show every extreme that they name: `tile_targets`: each row holds 8 different apex-latitude block indices. For every magnetic cell line_levels[0] < line_levels[1]; line_levels[0] is below 32.
All inputs are finite; a program needn't handle non-finite values.
Results may differ from the reference program's by a relative error of at most 0.0029.
Values may be sent and summed in bfloat16 or wider, within the bound.
No kernel may reach another device: no remote copies, remote signals or barrier semaphores. Data moves between devices by JAX's collectives and lax.ppermute only.
A program may use at most 128 MiB of HBM per device.

```python
import math
import jax
import jax.numpy as jnp
from jax import lax

L = 64
GC = 1024
MR = 8
MW = 128
KT = 8
MC = 1024
NGEO = 131072
NTILE = 1024
NMLAT = 128
NMLON = 1024
N_LAT = 16
N_LON = 8
DEVICES = 128


def draw_tile_targets(key, part):
    key = jax.random.fold_in(key, 23)
    scores = jax.random.randint(key, (DEVICES, N_LAT), 0, 1 << 20) * N_LAT + jnp.arange(N_LAT, dtype=jnp.int32)[None, :]
    order = jnp.argsort(scores, axis=1)
    return order[:, :KT].astype(jnp.int32)


def draw_line_levels(key, part):
    key = jax.random.fold_in(key, 11)
    first_key, second_key = jax.random.split(key)
    low_level = jax.random.randint(first_key, (NMLAT, NMLON), 0, L // 2)
    spans = jax.random.randint(second_key, (NMLAT, NMLON), 1, L + 1)
    high_level = jnp.minimum(low_level + spans, L)
    return jnp.stack([low_level, high_level]).astype(jnp.int32)


def block_scale(own_key, extent, cuts, smallest, largest):
    level, own = 1.0, jax.random.fold_in(own_key, 6)
    for dim, parts in cuts:
        steps = jnp.exp(jax.random.uniform(jax.random.fold_in(own, dim), (parts,), jnp.float32, smallest / len(cuts), largest / len(cuts)))
        level = level * jnp.repeat(steps, extent[dim] // parts).reshape([-1 if axis == dim else 1 for axis in range(len(extent))])
    return level


def normal_values(key, extent, spread, most, cuts=(), held_as=jnp.bfloat16):
    factor_of = block_scale(key, extent, cuts, -0.22, 0.18) if cuts else 1.0
    drawn = jax.random.normal(key, extent, jnp.float32) * spread * factor_of
    return jnp.minimum(jnp.maximum(drawn, -most), most).astype(held_as)


def setup_inputs(seed: int = 0) -> dict:
    arg_keys = jax.random.split(jax.random.key(seed), 8)
    return {
        "conductivity": jnp.clip(jnp.exp(math.log(2.0) - 2.306499 * jax.random.uniform(arg_keys[0], (2, L, NGEO), jnp.float32) ** block_scale(arg_keys[0], (2, L, NGEO), ((2, 128),), -0.2, 0.2)), 0.19921875, 2.0).astype(jnp.bfloat16),
        "wind_terms": normal_values(arg_keys[1], (4, L, NGEO), 1.0, 6.0, ((2, 128),)),
        "correlation_tiles": normal_values(arg_keys[2], (NTILE, MC, GC), GC ** -0.5, 0.1875, ((0, 128),)),
        "tile_targets": draw_tile_targets(jax.random.fold_in(arg_keys[7], 71), 0),
        "level_weights": jnp.clip(jnp.exp(jax.random.uniform(arg_keys[4], (L,), jnp.float32, math.log(0.02), math.log(0.2))), 0.02, 0.2),
        "line_levels": draw_line_levels(jax.random.fold_in(arg_keys[7], 71), 0),
        "potential": normal_values(arg_keys[6], (NMLAT, NMLON), 1.0, 6.0, ((0, 16), (1, 8)), jnp.float32),
    }


HIGHEST = lax.Precision.HIGHEST


def line_weights(ranges, level_weights):
    levels = jnp.arange(level_weights.shape[0], dtype=jnp.int32)[:, None]
    low_level = jnp.expand_dims(ranges[0], -2)
    high_level = jnp.expand_dims(ranges[1], -2)
    inside = (levels >= low_level) & (levels < high_level)
    return jnp.where(inside, level_weights[:, None], jnp.float32(0.0))


def assemble(extended, row_count, col_count):
    def cells_at(row_step, col_step):
        return extended[:, 1 + row_step:1 + row_step + row_count, 1 + col_step:1 + col_step + col_count]

    center = cells_at(0, 0)
    eastern = cells_at(0, 1)
    western = cells_at(0, -1)
    northern = cells_at(1, 0)
    southern = cells_at(-1, 0)
    north_east = cells_at(1, 1)
    north_west = cells_at(1, -1)
    south_east = cells_at(-1, 1)
    south_west = cells_at(-1, -1)
    east_coef = 0.5 * (center[0] + eastern[0])
    west_coef = 0.5 * (center[0] + western[0])
    north_coef = 0.5 * (center[0] + northern[0])
    south_coef = 0.5 * (center[0] + southern[0])
    ne_coef = 0.25 * (north_east[1] - center[1])
    nw_coef = -0.25 * (north_west[1] - center[1])
    se_coef = -0.25 * (south_east[1] - center[1])
    sw_coef = 0.25 * (south_west[1] - center[1])
    center_coef = -(east_coef + west_coef + north_coef + south_coef + ne_coef + nw_coef + se_coef + sw_coef)
    stencil = jnp.stack([center_coef, east_coef, west_coef, north_coef, south_coef, ne_coef, nw_coef, se_coef, sw_coef])
    zonal_part = (eastern[4] - eastern[3]) - (western[4] - western[3])
    merid_part = (southern[2] + southern[5]) - (northern[2] + northern[5])
    source_term = 0.5 * zonal_part + 0.5 * merid_part
    electric = jnp.stack([-0.5 * (eastern[6] - western[6]), -0.5 * (northern[6] - southern[6])])
    return stencil, source_term, electric


def to_blocks(grid_planes):
    plane_count = grid_planes.shape[0]
    shaped = grid_planes.reshape(plane_count, N_LAT, MR, N_LON, MW)
    return jnp.transpose(shaped, (1, 3, 0, 2, 4)).reshape(N_LAT, N_LON, plane_count, MR * MW)


def reference(conductivity, wind_terms, correlation_tiles, tile_targets, level_weights, line_levels, potential):
    devices = N_LAT * N_LON
    fields = jnp.concatenate([conductivity, wind_terms], 0)
    planes = fields.shape[0]
    flat_blocks = jnp.transpose(fields.reshape(planes * L, devices, GC), (1, 0, 2))
    tile_blocks = correlation_tiles.reshape(devices, KT, MR * MW, GC)
    device_ids = jnp.arange(devices, dtype=jnp.int32)

    def forward(carried, scanned):
        field_block, tiles_here, targets, device = scanned
        partial_value = lax.dot_general(field_block, tiles_here, (((1,), (2,)), ((), ())), preferred_element_type=jnp.float32)
        lon_index = device % N_LON
        carried = carried.at[targets, lon_index].add(jnp.transpose(partial_value, (1, 0, 2)))
        return carried, None

    initial = jnp.zeros((N_LAT, N_LON, planes * L, MR * MW), jnp.float32)
    regridded, unused = lax.scan(forward, initial, (flat_blocks, tile_blocks, tile_targets, device_ids))
    ranges = jnp.moveaxis(to_blocks(line_levels), 2, 0)
    weights = line_weights(ranges, level_weights)
    integrated = jnp.einsum("bjflc,bjlc->bjfc", regridded.reshape(N_LAT, N_LON, planes, L, MR * MW), weights, precision=HIGHEST)
    mag_grid = jnp.transpose(integrated.reshape(N_LAT, N_LON, planes, MR, MW), (2, 0, 3, 1, 4)).reshape(planes, N_LAT * MR, N_LON * MW)
    combined = mag_grid + mag_grid[:, ::-1, :]
    stacked = jnp.concatenate([combined, potential[None]], 0)
    extended = jnp.pad(stacked, ((0, 0), (1, 1), (0, 0)))
    extended = jnp.concatenate([extended[:, :, -1:], extended, extended[:, :, :1]], 2)
    stencil, source_term, electric = assemble(extended, N_LAT * MR, N_LON * MW)
    electric_blocks = to_blocks(electric.astype(jnp.bfloat16))

    def backward(carried, scanned):
        tiles_here, targets, device = scanned
        chosen = electric_blocks[targets, device % N_LON]
        result = lax.dot_general(chosen, tiles_here, (((0, 2), (0, 1)), ((), ())), preferred_element_type=jnp.float32)
        return carried, result

    unused_carry, geo_blocks = lax.scan(backward, jnp.float32(0.0), (tile_blocks, tile_targets, device_ids))
    geo_field = jnp.transpose(geo_blocks, (1, 0, 2)).reshape(2, devices * GC)
    return stencil, source_term, geo_field
```

```python
import functools

import jax
import jax.numpy as jnp
from jax import lax
from jax.experimental import pallas as pl
from jax.experimental.pallas import tpu as pltpu
from jax.sharding import PartitionSpec as P

RADIX = 128.0
ROWS, COLS = 8, 128
SUM_ROWS = 40


def pack_kernel(levels_ref, potential_ref, out_ref):
    packed = levels_ref[0].astype(jnp.float32) * RADIX + levels_ref[1].astype(jnp.float32)
    potential = potential_ref[...]
    for target in range(out_ref.shape[0]):
        out_ref[target, 0:ROWS, :] = packed
        out_ref[target, ROWS : 2 * ROWS, :] = potential


def pack(line_levels, potential, n_lat):
    return pl.pallas_call(
        pack_kernel,
        out_shape=jax.ShapeDtypeStruct((n_lat, 2 * ROWS, COLS), jnp.float32),
        in_specs=[pl.BlockSpec(memory_space=pltpu.VMEM)] * 2,
        out_specs=pl.BlockSpec(memory_space=pltpu.VMEM),
        name="pack_levels_potential",
    )(line_levels, potential)


def row_above(block, edge):
    rows = lax.broadcasted_iota(jnp.int32, block.shape, 0)
    return jnp.where(rows == ROWS - 1, edge, pltpu.roll(block, ROWS - 1, 0))


def row_below(block, edge):
    rows = lax.broadcasted_iota(jnp.int32, block.shape, 0)
    return jnp.where(rows == 0, edge, pltpu.roll(block, 1, 0))


def forward_kernel(
    targets, level_weights, conductivity, wind, gathered, tiles_hbm, out_ref, tiles, fields, weights, plain, mirrored, sems
):
    tile_count, mag_cells, geo_cells = tiles.shape
    levels_n = conductivity.shape[1]
    n_lat = gathered.shape[0]
    copies = [
        pltpu.make_async_copy(tiles_hbm.at[k], tiles.at[k], sems.at[k]) for k in range(tile_count)
    ]
    for copy in copies:
        copy.start()

    for level in range(levels_n):
        weights[level : level + 1, :] = jnp.full((1, COLS), level_weights[level], jnp.float32)
    fields[0:levels_n, :] = conductivity[0]
    fields[levels_n : 2 * levels_n, :] = conductivity[1]
    first, second, third, fourth = (wind[i].astype(jnp.float32) for i in range(4))
    fields[2 * levels_n : 3 * levels_n, :] = (third - second).astype(jnp.bfloat16)
    fields[3 * levels_n : 4 * levels_n, :] = (first + fourth).astype(jnp.bfloat16)
    plain[...] = jnp.zeros_like(plain)
    mirrored[...] = jnp.zeros_like(mirrored)
    level_of = lax.broadcasted_iota(jnp.int32, (levels_n, COLS), 0).astype(jnp.float32)

    chunk = 2 * COLS
    for k in range(tile_count):
        copies[k].wait()
        target = targets[0, k]
        opposite = n_lat - 1 - target
        for start in range(0, mag_cells, chunk):
            partial_value = lax.dot_general(
                fields[...],
                tiles[k, start : start + chunk, :],
                (((1,), (1,)), ((), ())),
                preferred_element_type=jnp.float32,
            )
            for piece in range(chunk // COLS):
                row = start // COLS + piece
                bounds = gathered[target, row : row + 1, :]
                low = jnp.floor(bounds * (1.0 / RADIX))
                high = bounds - low * RADIX
                inside = (level_of >= low) & (level_of < high)
                weight = jnp.where(inside, weights[...], 0.0)
                for f in range(4):
                    part = partial_value[
                        f * levels_n : (f + 1) * levels_n, piece * COLS : (piece + 1) * COLS
                    ]
                    total = jnp.sum(part * weight, axis=0, keepdims=True)
                    plain[target, f, row : row + 1, :] = total
                    mirrored[opposite, f, ROWS - 1 - row : ROWS - row, :] = total

    combined = [[plain[b, f] + mirrored[b, f] for f in range(4)] for b in range(n_lat)]
    nothing = jnp.zeros((1, COLS), jnp.float32)
    for b in range(n_lat):
        def edges(f):
            above = combined[b + 1][f][0:1] if b + 1 < n_lat else nothing
            below = combined[b - 1][f][ROWS - 1 : ROWS] if b > 0 else nothing
            return below, above

        merid = combined[b][3]
        below, above = edges(3)
        out_ref[b, 0:8, :] = combined[b][0]
        out_ref[b, 8:16, :] = combined[b][1]
        out_ref[b, 16:24, :] = combined[b][2]
        out_ref[b, 24:32, :] = row_below(merid, below) - row_above(merid, above)
        below0, above0 = edges(0)
        below1, above1 = edges(1)
        out_ref[b, 32:33, :] = below0
        out_ref[b, 33:34, :] = above0
        out_ref[b, 34:35, :] = below1
        out_ref[b, 35:36, :] = above1
        out_ref[b, 36:40, :] = jnp.zeros((4, COLS), jnp.float32)


def forward(targets, level_weights, conductivity, wind, gathered, tiles):
    n_lat = gathered.shape[0]
    levels_n, geo_cells = conductivity.shape[1:]
    smem = pl.BlockSpec(memory_space=pltpu.SMEM)
    vmem = pl.BlockSpec(memory_space=pltpu.VMEM)
    return pl.pallas_call(
        forward_kernel,
        out_shape=(
            jax.ShapeDtypeStruct((n_lat, SUM_ROWS, COLS), jnp.float32),
            pltpu.VMEM(tiles.shape, tiles.dtype),
        ),
        in_specs=[smem, smem, vmem, vmem, vmem, pl.BlockSpec(memory_space=pl.ANY)],
        out_specs=(vmem, vmem),
        scratch_shapes=[
            pltpu.VMEM((4 * levels_n, geo_cells), jnp.bfloat16),
            pltpu.VMEM((levels_n, COLS), jnp.float32),
            pltpu.VMEM((n_lat, 4, ROWS, COLS), jnp.float32),
            pltpu.VMEM((n_lat, 4, ROWS, COLS), jnp.float32),
            pltpu.SemaphoreType.DMA((tiles.shape[0],)),
        ],
        compiler_params=pltpu.CompilerParams(vmem_limit_bytes=40 * 2**20),
        cost_estimate=pl.CostEstimate(
            flops=2 * 4 * levels_n * tiles.size, bytes_accessed=2 * tiles.size, transcendentals=0
        ),
        name="regrid_integrate",
    )(targets, level_weights, conductivity, wind, gathered, tiles)


def backward_kernel(targets, gathered, west, east, tiles, out_ref, zonal, merid, rows_ref):
    tile_count, mag_cells, geo_cells = tiles.shape
    n_lat = gathered.shape[0]
    lanes = lax.broadcasted_iota(jnp.int32, (ROWS, COLS), 1)
    nothing = jnp.zeros((1, COLS), jnp.float32)
    for b in range(n_lat):
        here = gathered[b, ROWS : 2 * ROWS, :]
        eastern = jnp.where(
            lanes == COLS - 1, pltpu.roll(east[b, ROWS : 2 * ROWS, :], COLS - 1, 1), pltpu.roll(here, COLS - 1, 1)
        )
        western = jnp.where(
            lanes == 0, pltpu.roll(west[b, ROWS : 2 * ROWS, :], 1, 1), pltpu.roll(here, 1, 1)
        )
        above = gathered[b + 1, ROWS : ROWS + 1, :] if b + 1 < n_lat else nothing
        below = gathered[b - 1, 2 * ROWS - 1 : 2 * ROWS, :] if b > 0 else nothing
        zonal[b] = -0.5 * (eastern - western)
        merid[b] = -0.5 * (row_above(here, above) - row_below(here, below))
    rows_ref[...] = jnp.zeros_like(rows_ref)
    total = jnp.zeros((ROWS, geo_cells), jnp.float32)
    for k in range(tile_count):
        target = targets[0, k]
        for row in range(ROWS):
            columns = slice(row * COLS, (row + 1) * COLS)
            rows_ref[k, 0:1, columns] = zonal[target, row : row + 1, :]
            rows_ref[k, 1:2, columns] = merid[target, row : row + 1, :]
        total += jnp.dot(
            rows_ref[k].astype(jnp.bfloat16), tiles[k], preferred_element_type=jnp.float32
        )
    out_ref[...] = total[0:2]


def backward(targets, gathered, west, east, tiles):
    n_lat = gathered.shape[0]
    tile_count, mag_cells, geo_cells = tiles.shape
    smem = pl.BlockSpec(memory_space=pltpu.SMEM)
    vmem = pl.BlockSpec(memory_space=pltpu.VMEM)
    return pl.pallas_call(
        backward_kernel,
        out_shape=jax.ShapeDtypeStruct((2, geo_cells), jnp.float32),
        in_specs=[smem, vmem, vmem, vmem, vmem],
        out_specs=vmem,
        scratch_shapes=[
            pltpu.VMEM((n_lat, ROWS, COLS), jnp.float32),
            pltpu.VMEM((n_lat, ROWS, COLS), jnp.float32),
            pltpu.VMEM((tile_count, ROWS, mag_cells), jnp.float32),
        ],
        compiler_params=pltpu.CompilerParams(vmem_limit_bytes=40 * 2**20),
        cost_estimate=pl.CostEstimate(
            flops=16 * tiles.size, bytes_accessed=2 * tiles.size, transcendentals=0
        ),
        name="electric_to_geo",
    )(targets, gathered, west, east, tiles)


def stencil_kernel(sums, west, east, stencil_ref, source_ref):
    lanes = lax.broadcasted_iota(jnp.int32, (ROWS, COLS), 1)

    def eastward(begin):
        return jnp.where(
            lanes == COLS - 1,
            pltpu.roll(east[begin : begin + ROWS, :], COLS - 1, 1),
            pltpu.roll(sums[begin : begin + ROWS, :], COLS - 1, 1),
        )

    def westward(begin):
        return jnp.where(
            lanes == 0,
            pltpu.roll(west[begin : begin + ROWS, :], 1, 1),
            pltpu.roll(sums[begin : begin + ROWS, :], 1, 1),
        )

    edge, edge_east, edge_west = sums[32:40, :], eastward(32), westward(32)
    center0, center1 = sums[0:8, :], sums[8:16, :]
    east1, west1 = eastward(8), westward(8)
    east_coef = 0.5 * (center0 + eastward(0))
    west_coef = 0.5 * (center0 + westward(0))
    north_coef = 0.5 * (center0 + row_above(center0, edge[1:2]))
    south_coef = 0.5 * (center0 + row_below(center0, edge[0:1]))
    ne_coef = 0.25 * (row_above(east1, edge_east[3:4]) - center1)
    nw_coef = -0.25 * (row_above(west1, edge_west[3:4]) - center1)
    se_coef = -0.25 * (row_below(east1, edge_east[2:3]) - center1)
    sw_coef = 0.25 * (row_below(west1, edge_west[2:3]) - center1)
    others = [east_coef, west_coef, north_coef, south_coef, ne_coef, nw_coef, se_coef, sw_coef]
    stencil_ref[0] = -sum(others[1:], others[0])
    for i, coef in enumerate(others):
        stencil_ref[i + 1] = coef
    source_ref[...] = 0.5 * (eastward(16) - westward(16)) + 0.5 * sums[24:32, :]


def stencil_source(sums, west, east):
    vmem = pl.BlockSpec(memory_space=pltpu.VMEM)
    return pl.pallas_call(
        stencil_kernel,
        out_shape=(
            jax.ShapeDtypeStruct((9, ROWS, COLS), jnp.float32),
            jax.ShapeDtypeStruct((ROWS, COLS), jnp.float32),
        ),
        in_specs=[vmem] * 3,
        out_specs=(vmem, vmem),
        name="stencil_source",
    )(sums, west, east)


def lon_neighbours(block):
    count = lax.axis_size("lon")
    from_west = [(i, (i + 1) % count) for i in range(count)]
    from_east = [((i + 1) % count, i) for i in range(count)]
    return lax.ppermute(block, "lon", from_west), lax.ppermute(block, "lon", from_east)


def per_device(
    conductivity, wind_terms, correlation_tiles, tile_targets, level_weights, line_levels, potential
):
    n_lat = lax.axis_size("lat")
    packed = pack(line_levels, potential, n_lat)
    gathered = lax.all_to_all(packed, "lat", 0, 0, tiled=True)
    west, east = lon_neighbours(gathered)
    sends, tiles = forward(
        tile_targets, level_weights, conductivity, wind_terms, gathered, correlation_tiles
    )
    received = lax.all_to_all(sends, "lat", 0, 0, tiled=True)
    sums = jnp.sum(received, axis=0)
    sums_west, sums_east = lon_neighbours(sums)
    geo_field = backward(tile_targets, gathered, west, east, tiles)
    stencil, source_term = stencil_source(sums, sums_west, sums_east)
    return stencil, source_term, geo_field


def solution(mesh):
    in_specs = (
        P(None, None, ("lat", "lon")),
        P(None, None, ("lat", "lon")),
        P(("lat", "lon"), None, None),
        P(("lat", "lon"), None),
        P(),
        P(None, "lat", "lon"),
        P("lat", "lon"),
    )
    out_specs = (P(None, "lat", "lon"), P("lat", "lon"), P(None, ("lat", "lon")))
    return jax.shard_map(
        per_device, mesh=mesh, in_specs=in_specs, out_specs=out_specs, check_vma=False
    )
```

```python
import functools

import jax
import jax.numpy as jnp
from jax import lax
from jax.experimental import pallas as pl
from jax.experimental.pallas import tpu as pltpu
from jax.sharding import PartitionSpec as P

RADIX = 128.0
ROWS, COLS = 8, 128
SUM_ROWS = 48
SCOPED = 24 * 2**20
SMALL = 8 * 2**20
CHUNK = 2 * COLS
VMEM_SPEC = pl.BlockSpec(memory_space=pltpu.VMEM)
HBM_SPEC = pl.BlockSpec(memory_space=pltpu.HBM)
SMEM_SPEC = pl.BlockSpec(memory_space=pltpu.SMEM)


def pack_kernel(levels_ref, potential_ref, out_ref):
    packed = levels_ref[0].astype(jnp.float32) * RADIX + levels_ref[1].astype(jnp.float32)
    potential = potential_ref[...]
    for target in range(out_ref.shape[0]):
        out_ref[target, 0:ROWS, :] = packed
        out_ref[target, ROWS : 2 * ROWS, :] = potential


def pack(line_levels, potential, n_lat):
    return pl.pallas_call(
        pack_kernel,
        out_shape=pltpu.VMEM((n_lat, 2 * ROWS, COLS), jnp.float32),
        in_specs=[VMEM_SPEC] * 2,
        out_specs=VMEM_SPEC,
        name="pack_levels_potential",
    )(line_levels, potential)


def row_above(block, edge):
    rows = lax.broadcasted_iota(jnp.int32, block.shape, 0)
    return jnp.where(rows == ROWS - 1, edge, pltpu.roll(block, ROWS - 1, 0))


def row_below(block, edge):
    rows = lax.broadcasted_iota(jnp.int32, block.shape, 0)
    return jnp.where(rows == 0, edge, pltpu.roll(block, 1, 0))


def in_vmem(array):
    return pltpu.with_memory_space_constraint(array, pltpu.VMEM)


def in_hbm(array):
    return pltpu.with_memory_space_constraint(array, pltpu.HBM)


def product_kernel(
    conductivity_hbm, wind_hbm, tiles_hbm, near_plain, near_wind, far_plain_hbm, far_wind_hbm,
    fields, conductivity, wind, tiles, far_plain, far_wind, sems, far_sems,
):
    tile_count, mag_cells, geo_cells = tiles.shape
    levels_n = conductivity.shape[1]
    near_count = near_plain.shape[0]
    order = list(range(near_count, tile_count)) + list(range(near_count))
    field_copies = [
        pltpu.make_async_copy(conductivity_hbm, conductivity, sems.at[tile_count]),
        pltpu.make_async_copy(wind_hbm, wind, sems.at[tile_count + 1]),
    ]
    tile_copies = {
        k: pltpu.make_async_copy(tiles_hbm.at[k], tiles.at[k], sems.at[k]) for k in order
    }
    for copy in field_copies + list(tile_copies.values()):
        copy.start()
    for copy in field_copies:
        copy.wait()
    fields[0:levels_n, :] = conductivity[0]
    fields[levels_n : 2 * levels_n, :] = conductivity[1]
    first, second, third, fourth = (wind[i].astype(jnp.float32) for i in range(4))
    fields[2 * levels_n : 3 * levels_n, :] = (third - second).astype(jnp.bfloat16)
    fields[3 * levels_n : 4 * levels_n, :] = (first + fourth).astype(jnp.bfloat16)
    far_copies = []
    for k in order:
        tile_copies[k].wait()
        near, i = k < near_count, k if k < near_count else k - near_count
        plain_out, wind_out = (near_plain, near_wind) if near else (far_plain, far_wind)
        for start in range(0, mag_cells, CHUNK):
            columns = slice(start, start + CHUNK)
            value = lax.dot_general(
                fields[...],
                tiles[k, columns, :],
                (((1,), (1,)), ((), ())),
                preferred_element_type=jnp.float32,
            )
            plain_out[i, :, columns] = value[: 2 * levels_n].astype(jnp.bfloat16)
            wind_out[i, :, columns] = value[2 * levels_n :]
        if not near:
            copies = [
                pltpu.make_async_copy(far_plain.at[i], far_plain_hbm.at[i], far_sems.at[2 * i]),
                pltpu.make_async_copy(far_wind.at[i], far_wind_hbm.at[i], far_sems.at[2 * i + 1]),
            ]
            for copy in copies:
                copy.start()
            far_copies += copies
    for copy in far_copies:
        copy.wait()


def product(conductivity, wind, tiles, near_count):
    levels_n, geo_cells = conductivity.shape[1:]
    tile_count, mag_cells = tiles.shape[:2]
    far_count = tile_count - near_count
    near_shape, far_shape = ((count, 2 * levels_n, mag_cells) for count in (near_count, far_count))
    return pl.pallas_call(
        product_kernel,
        out_shape=(
            pltpu.VMEM(near_shape, jnp.bfloat16),
            pltpu.VMEM(near_shape, jnp.float32),
            pltpu.HBM(far_shape, jnp.bfloat16),
            pltpu.HBM(far_shape, jnp.float32),
        ),
        in_specs=[HBM_SPEC] * 3,
        out_specs=(VMEM_SPEC, VMEM_SPEC, HBM_SPEC, HBM_SPEC),
        scratch_shapes=[
            pltpu.VMEM((4 * levels_n, geo_cells), jnp.bfloat16),
            pltpu.VMEM(conductivity.shape, conductivity.dtype),
            pltpu.VMEM(wind.shape, wind.dtype),
            pltpu.VMEM(tiles.shape, tiles.dtype),
            pltpu.VMEM(far_shape, jnp.bfloat16),
            pltpu.VMEM(far_shape, jnp.float32),
            pltpu.SemaphoreType.DMA((tile_count + 2,)),
            pltpu.SemaphoreType.DMA((2 * far_count,)),
        ],
        compiler_params=pltpu.CompilerParams(vmem_limit_bytes=SCOPED),
        cost_estimate=pl.CostEstimate(
            flops=2 * 4 * levels_n * tiles.size, bytes_accessed=2 * tiles.size, transcendentals=0
        ),
        name="regrid_product",
    )(conductivity, wind, tiles)


def integral_kernel(
    targets, level_weights, gathered, near_plain, near_wind, far_plain_hbm, far_wind_hbm, combined, edges,
    weights, plain, mirrored, far_plain, far_wind, sems,
):
    near_count, far_count = near_plain.shape[0], far_plain.shape[0]
    levels_n = level_weights.shape[0]
    n_lat = gathered.shape[0]
    copies = [
        (
            pltpu.make_async_copy(far_plain_hbm.at[i], far_plain.at[i], sems.at[2 * i]),
            pltpu.make_async_copy(far_wind_hbm.at[i], far_wind.at[i], sems.at[2 * i + 1]),
        )
        for i in range(far_count)
    ]
    for pair in copies:
        for copy in pair:
            copy.start()
    for level in range(levels_n):
        weights[level : level + 1, :] = jnp.full((1, COLS), level_weights[level], jnp.float32)
    plain[...] = jnp.zeros_like(plain)
    mirrored[...] = jnp.zeros_like(mirrored)
    level_of = lax.broadcasted_iota(jnp.int32, (levels_n, COLS), 0).astype(jnp.float32)
    for k in range(near_count + far_count):
        if k >= near_count:
            for copy in copies[k - near_count]:
                copy.wait()
        near, i = k < near_count, k if k < near_count else k - near_count
        planes = (near_plain, near_wind) if near else (far_plain, far_wind)
        target = targets[0, k]
        for row in range(ROWS):
            bounds = gathered[target, row : row + 1, :]
            low = jnp.floor(bounds * (1.0 / RADIX))
            high = bounds - low * RADIX
            inside = (level_of >= low) & (level_of < high)
            weight = jnp.where(inside, weights[...], 0.0)
            for f in range(4):
                rows = slice(f % 2 * levels_n, (f % 2 + 1) * levels_n)
                part = planes[f // 2][i, rows, row * COLS : (row + 1) * COLS]
                total = jnp.sum(part.astype(jnp.float32) * weight, axis=0, keepdims=True)
                plain[target, f, row : row + 1, :] = total
                mirrored[n_lat - 1 - target, f, ROWS - 1 - row : ROWS - row, :] = total

    lanes = lax.broadcasted_iota(jnp.int32, (ROWS, COLS), 1)
    for f in range(4):
        for b in range(n_lat):
            combined[b, f] = plain[b, f] + mirrored[b, f]

    def both_edges(block_of):
        edge = jnp.zeros((ROWS, COLS), jnp.float32)
        for b in range(n_lat):
            block = block_of(b)
            edge = jnp.where(lanes == 2 * b, pltpu.roll(block, 2 * b, 1), edge)
            edge = jnp.where(lanes == 2 * b + 1, pltpu.roll(block, 2 * b + 2, 1), edge)
        return edge

    for f in range(3):
        edges[f * ROWS : (f + 1) * ROWS, :] = both_edges(lambda b: combined[b, f])
    edges[3 * ROWS : 4 * ROWS, :] = both_edges(lambda b: gathered[b, ROWS : 2 * ROWS, :])


def integral(targets, level_weights, gathered, near, far):
    far_shape = far[0].shape
    n_lat = gathered.shape[0]
    return pl.pallas_call(
        integral_kernel,
        out_shape=(
            pltpu.VMEM((n_lat, 4, ROWS, COLS), jnp.float32),
            pltpu.VMEM((4 * ROWS, COLS), jnp.float32),
        ),
        in_specs=[SMEM_SPEC] * 2 + [VMEM_SPEC] * 3 + [HBM_SPEC] * 2,
        out_specs=(VMEM_SPEC, VMEM_SPEC),
        scratch_shapes=[
            pltpu.VMEM((level_weights.shape[0], COLS), jnp.float32),
            pltpu.VMEM((n_lat, 4, ROWS, COLS), jnp.float32),
            pltpu.VMEM((n_lat, 4, ROWS, COLS), jnp.float32),
            pltpu.VMEM(far_shape, jnp.bfloat16),
            pltpu.VMEM(far_shape, jnp.float32),
            pltpu.SemaphoreType.DMA((2 * far_shape[0],)),
        ],
        compiler_params=pltpu.CompilerParams(vmem_limit_bytes=SCOPED),
        cost_estimate=pl.CostEstimate(
            flops=6 * near[0].size, bytes_accessed=16 * near[0].size, transcendentals=0
        ),
        name="level_integral",
    )(targets, level_weights, in_vmem(gathered), *map(in_vmem, near), *map(in_hbm, far))


def assemble_kernel(combined, west, east, out_ref):
    n_lat = combined.shape[0]
    lanes = lax.broadcasted_iota(jnp.int32, (ROWS, COLS), 1)
    beyond = [
        jnp.where(lanes % 2 == 0, east[f * ROWS : (f + 1) * ROWS, :], west[f * ROWS : (f + 1) * ROWS, :])
        for f in range(3)
    ]
    corners = [pltpu.roll(beyond[1], (COLS - 2 * b) % COLS, 1) for b in range(n_lat)]
    nothing = jnp.zeros((1, COLS), jnp.float32)
    for b in range(n_lat):
        def below(blocks):
            return blocks(b - 1)[ROWS - 1 : ROWS] if b > 0 else nothing

        def above(blocks):
            return blocks(b + 1)[0:1] if b + 1 < n_lat else nothing

        merid = combined[b, 3]
        for f in range(3):
            out_ref[b, f * ROWS : (f + 1) * ROWS, :] = combined[b, f]
        out_ref[b, 24:32, :] = row_below(merid, below(lambda i: combined[i, 3])) - row_above(
            merid, above(lambda i: combined[i, 3])
        )
        out_ref[b, 32:33, :] = below(lambda i: combined[i, 0])
        out_ref[b, 33:34, :] = above(lambda i: combined[i, 0])
        out_ref[b, 34:35, :] = below(lambda i: combined[i, 1])
        out_ref[b, 35:36, :] = above(lambda i: combined[i, 1])
        out_ref[b, 36:37, :] = below(lambda i: corners[i])
        out_ref[b, 37:38, :] = above(lambda i: corners[i])
        out_ref[b, 38:40, :] = jnp.zeros((2, COLS), jnp.float32)
        columns = jnp.zeros((ROWS, COLS), jnp.float32)
        for f in range(3):
            moved = pltpu.roll(beyond[f], (COLS + 2 * f - 2 * b) % COLS, 1)
            columns = jnp.where((lanes >= 2 * f) & (lanes < 2 * f + 2), moved, columns)
        out_ref[b, 40:48, :] = columns


def assemble(combined, west, east):
    return pl.pallas_call(
        assemble_kernel,
        out_shape=jax.ShapeDtypeStruct((combined.shape[0], SUM_ROWS, COLS), jnp.float32),
        in_specs=[VMEM_SPEC] * 3,
        out_specs=VMEM_SPEC,
        compiler_params=pltpu.CompilerParams(vmem_limit_bytes=SMALL),
        name="assemble_sends",
    )(in_vmem(combined), in_vmem(west), in_vmem(east))


def backward_kernel(targets, gathered, west, east, tiles_hbm, out_ref, zonal, merid, rows_ref, tiles, sems):
    n_lat = gathered.shape[0]
    tile_count = tiles.shape[0]
    copies = [
        pltpu.make_async_copy(tiles_hbm.at[k], tiles.at[k], sems.at[k]) for k in range(tile_count)
    ]
    for copy in copies:
        copy.start()
    lanes = lax.broadcasted_iota(jnp.int32, (ROWS, COLS), 1)
    nothing = jnp.zeros((1, COLS), jnp.float32)
    west_edges, east_edges = west[3 * ROWS : 4 * ROWS, :], east[3 * ROWS : 4 * ROWS, :]
    for b in range(n_lat):
        here = gathered[b, ROWS : 2 * ROWS, :]
        shift = COLS - 1 - 2 * b
        eastern = jnp.where(
            lanes == COLS - 1, pltpu.roll(east_edges, shift, 1), pltpu.roll(here, COLS - 1, 1)
        )
        western = jnp.where(lanes == 0, pltpu.roll(west_edges, shift, 1), pltpu.roll(here, 1, 1))
        above = gathered[b + 1, ROWS : ROWS + 1, :] if b + 1 < n_lat else nothing
        below = gathered[b - 1, 2 * ROWS - 1 : 2 * ROWS, :] if b > 0 else nothing
        zonal[b] = -0.5 * (eastern - western)
        merid[b] = -0.5 * (row_above(here, above) - row_below(here, below))
    rows_ref[...] = jnp.zeros_like(rows_ref)
    for k in range(tile_count):
        target = targets[0, k]
        for row in range(ROWS):
            columns = slice(row * COLS, (row + 1) * COLS)
            rows_ref[k, 0:1, columns] = zonal[target, row : row + 1, :]
            rows_ref[k, 1:2, columns] = merid[target, row : row + 1, :]
    total = jnp.zeros((ROWS, tiles.shape[2]), jnp.float32)
    for k in range(tile_count):
        copies[k].wait()
        total += jnp.dot(
            rows_ref[k].astype(jnp.bfloat16), tiles[k], preferred_element_type=jnp.float32
        )
    out_ref[...] = total[0:2]


def backward(targets, gathered, west, east, tiles):
    n_lat = gathered.shape[0]
    tile_count, mag_cells, geo_cells = tiles.shape
    return pl.pallas_call(
        backward_kernel,
        out_shape=jax.ShapeDtypeStruct((2, geo_cells), jnp.float32),
        in_specs=[SMEM_SPEC, VMEM_SPEC, VMEM_SPEC, VMEM_SPEC, HBM_SPEC],
        out_specs=VMEM_SPEC,
        scratch_shapes=[
            pltpu.VMEM((n_lat, ROWS, COLS), jnp.float32),
            pltpu.VMEM((n_lat, ROWS, COLS), jnp.float32),
            pltpu.VMEM((tile_count, ROWS, mag_cells), jnp.float32),
            pltpu.VMEM(tiles.shape, tiles.dtype),
            pltpu.SemaphoreType.DMA((tile_count,)),
        ],
        compiler_params=pltpu.CompilerParams(vmem_limit_bytes=SCOPED),
        cost_estimate=pl.CostEstimate(
            flops=16 * tiles.size, bytes_accessed=2 * tiles.size, transcendentals=0
        ),
        name="electric_to_geo",
    )(targets, in_vmem(gathered), in_vmem(west), in_vmem(east), tiles)


def stencil_kernel(received, stencil_ref, source_ref):
    sums = received[0]
    for source in range(1, received.shape[0]):
        sums += received[source]
    lanes = lax.broadcasted_iota(jnp.int32, (ROWS, COLS), 1)
    columns = sums[40:48]

    def eastward(block, beyond, lane):
        moved = pltpu.roll(beyond, COLS - 1 - lane, 1)
        return jnp.where(lanes == COLS - 1, moved, pltpu.roll(block, COLS - 1, 1))

    def westward(block, beyond, lane):
        moved = pltpu.roll(beyond, (COLS - lane) % COLS, 1)
        return jnp.where(lanes == 0, moved, pltpu.roll(block, 1, 1))

    center0, center1, zonal, merid, edge = (sums[i * ROWS : (i + 1) * ROWS] for i in range(5))
    corner = pltpu.roll(edge, ROWS - 2, 0)
    edge_east, edge_west = eastward(edge, corner, 0), westward(edge, corner, 1)
    east1, west1 = eastward(center1, columns, 2), westward(center1, columns, 3)
    east_coef = 0.5 * (center0 + eastward(center0, columns, 0))
    west_coef = 0.5 * (center0 + westward(center0, columns, 1))
    north_coef = 0.5 * (center0 + row_above(center0, edge[1:2]))
    south_coef = 0.5 * (center0 + row_below(center0, edge[0:1]))
    ne_coef = 0.25 * (row_above(east1, edge_east[3:4]) - center1)
    nw_coef = -0.25 * (row_above(west1, edge_west[3:4]) - center1)
    se_coef = -0.25 * (row_below(east1, edge_east[2:3]) - center1)
    sw_coef = 0.25 * (row_below(west1, edge_west[2:3]) - center1)
    others = [east_coef, west_coef, north_coef, south_coef, ne_coef, nw_coef, se_coef, sw_coef]
    stencil_ref[0] = -sum(others[1:], others[0])
    for i, coef in enumerate(others):
        stencil_ref[i + 1] = coef
    source_ref[...] = (
        0.5 * (eastward(zonal, columns, 4) - westward(zonal, columns, 5)) + 0.5 * merid
    )


def stencil_source(received):
    return pl.pallas_call(
        stencil_kernel,
        out_shape=(
            jax.ShapeDtypeStruct((9, ROWS, COLS), jnp.float32),
            jax.ShapeDtypeStruct((ROWS, COLS), jnp.float32),
        ),
        in_specs=[VMEM_SPEC],
        out_specs=(VMEM_SPEC, VMEM_SPEC),
        compiler_params=pltpu.CompilerParams(vmem_limit_bytes=SMALL),
        name="stencil_source",
    )(in_vmem(received))


def lon_neighbours(block):
    count = lax.axis_size("lon")
    from_west = [(i, (i + 1) % count) for i in range(count)]
    from_east = [((i + 1) % count, i) for i in range(count)]
    return lax.ppermute(block, "lon", from_west), lax.ppermute(block, "lon", from_east)


def per_device(
    conductivity, wind_terms, correlation_tiles, tile_targets, level_weights, line_levels, potential
):
    n_lat = lax.axis_size("lat")
    tiles = in_hbm(correlation_tiles)
    near_count = tiles.shape[0] // 2
    packed = pack(line_levels, potential, n_lat)
    gathered = lax.all_to_all(packed, "lat", 0, 0, tiled=True)
    near_plain, near_wind, far_plain, far_wind = product(in_hbm(conductivity), in_hbm(wind_terms), tiles, near_count)
    combined, edges = integral(tile_targets, level_weights, gathered, (near_plain, near_wind), (far_plain, far_wind))
    west, east = lon_neighbours(edges)
    sends = assemble(combined, west, east)
    received = lax.all_to_all(sends, "lat", 0, 0, tiled=True)
    geo_field = backward(tile_targets, gathered, west, east, tiles)
    stencil, source_term = stencil_source(received)
    return stencil, source_term, geo_field


def solution(mesh):
    in_specs = (
        P(None, None, ("lat", "lon")),
        P(None, None, ("lat", "lon")),
        P(("lat", "lon"), None, None),
        P(("lat", "lon"), None),
        P(),
        P(None, "lat", "lon"),
        P("lat", "lon"),
    )
    out_specs = (P(None, "lat", "lon"), P("lat", "lon"), P(None, ("lat", "lon")))
    return jax.shard_map(
        per_device, mesh=mesh, in_specs=in_specs, out_specs=out_specs, check_vma=False
    )
```

```python
import functools

import jax
import jax.numpy as jnp
from jax import lax
from jax.experimental import pallas as pl
from jax.experimental.pallas import tpu as pltpu
from jax.sharding import PartitionSpec as P

RADIX = 128.0
ROWS, COLS = 8, 128
SUM_ROWS = 48
SCOPED = 24 * 2**20
SMALL = 8 * 2**20
CHUNK = 2 * COLS
VMEM_SPEC = pl.BlockSpec(memory_space=pltpu.VMEM)
HBM_SPEC = pl.BlockSpec(memory_space=pltpu.HBM)
SMEM_SPEC = pl.BlockSpec(memory_space=pltpu.SMEM)


def pack_kernel(levels_ref, potential_ref, out_ref):
    packed = levels_ref[0].astype(jnp.float32) * RADIX + levels_ref[1].astype(jnp.float32)
    potential = potential_ref[...]
    for target in range(out_ref.shape[0]):
        out_ref[target, 0:ROWS, :] = packed
        out_ref[target, ROWS : 2 * ROWS, :] = potential


def pack(line_levels, potential, n_lat):
    return pl.pallas_call(
        pack_kernel,
        out_shape=pltpu.VMEM((n_lat, 2 * ROWS, COLS), jnp.float32),
        in_specs=[VMEM_SPEC] * 2,
        out_specs=VMEM_SPEC,
        name="pack_levels_potential",
    )(line_levels, potential)


def row_above(block, edge):
    rows = lax.broadcasted_iota(jnp.int32, block.shape, 0)
    return jnp.where(rows == ROWS - 1, edge, pltpu.roll(block, ROWS - 1, 0))


def row_below(block, edge):
    rows = lax.broadcasted_iota(jnp.int32, block.shape, 0)
    return jnp.where(rows == 0, edge, pltpu.roll(block, 1, 0))


def in_vmem(array):
    return pltpu.with_memory_space_constraint(array, pltpu.VMEM)


def in_hbm(array):
    return pltpu.with_memory_space_constraint(array, pltpu.HBM)


def product_kernel(
    conductivity_hbm, wind_hbm, tiles_hbm, near_plain, near_wind, far_plain_hbm, far_wind_hbm,
    fields, conductivity, wind, tiles, far_plain, far_wind, sems, far_sems,
):
    tile_count, mag_cells, geo_cells = tiles.shape
    levels_n = conductivity.shape[1]
    near_count = near_plain.shape[0]
    order = list(range(near_count, tile_count)) + list(range(near_count))
    field_copies = [
        pltpu.make_async_copy(conductivity_hbm, conductivity, sems.at[tile_count]),
        pltpu.make_async_copy(wind_hbm, wind, sems.at[tile_count + 1]),
    ]
    tile_copies = {
        k: pltpu.make_async_copy(tiles_hbm.at[k], tiles.at[k], sems.at[k]) for k in order
    }
    for copy in field_copies + list(tile_copies.values()):
        copy.start()
    for copy in field_copies:
        copy.wait()
    fields[0:levels_n, :] = conductivity[0]
    fields[levels_n : 2 * levels_n, :] = conductivity[1]
    first, second, third, fourth = (wind[i].astype(jnp.float32) for i in range(4))
    fields[2 * levels_n : 3 * levels_n, :] = (third - second).astype(jnp.bfloat16)
    fields[3 * levels_n : 4 * levels_n, :] = (first + fourth).astype(jnp.bfloat16)
    far_copies = []
    for k in order:
        tile_copies[k].wait()
        near, i = k < near_count, k if k < near_count else k - near_count
        plain_out, wind_out = (near_plain, near_wind) if near else (far_plain, far_wind)
        for start in range(0, mag_cells, CHUNK):
            columns = slice(start, start + CHUNK)
            value = lax.dot_general(
                fields[...],
                tiles[k, columns, :],
                (((1,), (1,)), ((), ())),
                preferred_element_type=jnp.float32,
            )
            plain_out[i, :, columns] = value[: 2 * levels_n].astype(jnp.bfloat16)
            wind_out[i, :, columns] = value[2 * levels_n :]
        if not near:
            copies = [
                pltpu.make_async_copy(far_plain.at[i], far_plain_hbm.at[i], far_sems.at[2 * i]),
                pltpu.make_async_copy(far_wind.at[i], far_wind_hbm.at[i], far_sems.at[2 * i + 1]),
            ]
            for copy in copies:
                copy.start()
            far_copies += copies
    for copy in far_copies:
        copy.wait()


def product(conductivity, wind, tiles, near_count):
    levels_n, geo_cells = conductivity.shape[1:]
    tile_count, mag_cells = tiles.shape[:2]
    far_count = tile_count - near_count
    near_shape, far_shape = ((count, 2 * levels_n, mag_cells) for count in (near_count, far_count))
    return pl.pallas_call(
        product_kernel,
        out_shape=(
            pltpu.VMEM(near_shape, jnp.bfloat16),
            pltpu.VMEM(near_shape, jnp.float32),
            pltpu.HBM(far_shape, jnp.bfloat16),
            pltpu.HBM(far_shape, jnp.float32),
        ),
        in_specs=[HBM_SPEC] * 3,
        out_specs=(VMEM_SPEC, VMEM_SPEC, HBM_SPEC, HBM_SPEC),
        scratch_shapes=[
            pltpu.VMEM((4 * levels_n, geo_cells), jnp.bfloat16),
            pltpu.VMEM(conductivity.shape, conductivity.dtype),
            pltpu.VMEM(wind.shape, wind.dtype),
            pltpu.VMEM(tiles.shape, tiles.dtype),
            pltpu.VMEM(far_shape, jnp.bfloat16),
            pltpu.VMEM(far_shape, jnp.float32),
            pltpu.SemaphoreType.DMA((tile_count + 2,)),
            pltpu.SemaphoreType.DMA((2 * far_count,)),
        ],
        compiler_params=pltpu.CompilerParams(vmem_limit_bytes=SCOPED),
        cost_estimate=pl.CostEstimate(
            flops=2 * 4 * levels_n * tiles.size, bytes_accessed=2 * tiles.size, transcendentals=0
        ),
        name="regrid_product",
    )(conductivity, wind, tiles)


def integral_kernel(
    targets, level_weights, gathered, near_plain, near_wind, far_plain_hbm, far_wind_hbm, combined, edges,
    weights, plain, mirrored, far_plain, far_wind, sems,
):
    near_count, far_count = near_plain.shape[0], far_plain.shape[0]
    levels_n = level_weights.shape[0]
    n_lat = gathered.shape[0]
    copies = [
        (
            pltpu.make_async_copy(far_plain_hbm.at[i], far_plain.at[i], sems.at[2 * i]),
            pltpu.make_async_copy(far_wind_hbm.at[i], far_wind.at[i], sems.at[2 * i + 1]),
        )
        for i in range(far_count)
    ]
    for pair in copies:
        for copy in pair:
            copy.start()
    for level in range(levels_n):
        weights[level : level + 1, :] = jnp.full((1, COLS), level_weights[level], jnp.float32)
    plain[...] = jnp.zeros_like(plain)
    mirrored[...] = jnp.zeros_like(mirrored)
    level_of = lax.broadcasted_iota(jnp.int32, (levels_n, COLS), 0).astype(jnp.float32)
    for k in range(near_count + far_count):
        if k >= near_count:
            for copy in copies[k - near_count]:
                copy.wait()
        near, i = k < near_count, k if k < near_count else k - near_count
        planes = (near_plain, near_wind) if near else (far_plain, far_wind)
        target = targets[0, k]
        for row in range(ROWS):
            bounds = gathered[target, row : row + 1, :]
            low = jnp.floor(bounds * (1.0 / RADIX))
            high = bounds - low * RADIX
            inside = (level_of >= low) & (level_of < high)
            weight = jnp.where(inside, weights[...], 0.0)
            for f in range(4):
                rows = slice(f % 2 * levels_n, (f % 2 + 1) * levels_n)
                part = planes[f // 2][i, rows, row * COLS : (row + 1) * COLS]
                total = jnp.sum(part.astype(jnp.float32) * weight, axis=0, keepdims=True)
                plain[target, f, row : row + 1, :] = total
                mirrored[n_lat - 1 - target, f, ROWS - 1 - row : ROWS - row, :] = total

    lanes = lax.broadcasted_iota(jnp.int32, (ROWS, COLS), 1)
    for f in range(4):
        for b in range(n_lat):
            combined[b, f] = plain[b, f] + mirrored[b, f]

    def both_edges(block_of):
        edge = jnp.zeros((ROWS, COLS), jnp.float32)
        for b in range(n_lat):
            block = block_of(b)
            edge = jnp.where(lanes == 2 * b, pltpu.roll(block, 2 * b, 1), edge)
            edge = jnp.where(lanes == 2 * b + 1, pltpu.roll(block, 2 * b + 2, 1), edge)
        return edge

    for f in range(3):
        edges[f * ROWS : (f + 1) * ROWS, :] = both_edges(lambda b: combined[b, f])
    edges[3 * ROWS : 4 * ROWS, :] = both_edges(lambda b: gathered[b, ROWS : 2 * ROWS, :])


def integral(targets, level_weights, gathered, near, far):
    far_shape = far[0].shape
    n_lat = gathered.shape[0]
    return pl.pallas_call(
        integral_kernel,
        out_shape=(
            pltpu.VMEM((n_lat, 4, ROWS, COLS), jnp.float32),
            pltpu.VMEM((4 * ROWS, COLS), jnp.float32),
        ),
        in_specs=[SMEM_SPEC] * 2 + [VMEM_SPEC] * 3 + [HBM_SPEC] * 2,
        out_specs=(VMEM_SPEC, VMEM_SPEC),
        scratch_shapes=[
            pltpu.VMEM((level_weights.shape[0], COLS), jnp.float32),
            pltpu.VMEM((n_lat, 4, ROWS, COLS), jnp.float32),
            pltpu.VMEM((n_lat, 4, ROWS, COLS), jnp.float32),
            pltpu.VMEM(far_shape, jnp.bfloat16),
            pltpu.VMEM(far_shape, jnp.float32),
            pltpu.SemaphoreType.DMA((2 * far_shape[0],)),
        ],
        compiler_params=pltpu.CompilerParams(vmem_limit_bytes=SCOPED),
        cost_estimate=pl.CostEstimate(
            flops=6 * near[0].size, bytes_accessed=16 * near[0].size, transcendentals=0
        ),
        name="level_integral",
    )(targets, level_weights, in_vmem(gathered), *map(in_vmem, near), *map(in_hbm, far))


def assemble_kernel(combined, inside, across, out_ref):
    n_lat = combined.shape[0]
    lanes = lax.broadcasted_iota(jnp.int32, (ROWS, COLS), 1)
    beyond = []
    for f in range(3):
        rows = slice(f * ROWS, (f + 1) * ROWS)
        west, east = west_and_east(inside[rows, :], across[rows, :])
        beyond.append(jnp.where(lanes % 2 == 0, east, west))
    corners = [pltpu.roll(beyond[1], (COLS - 2 * b) % COLS, 1) for b in range(n_lat)]
    nothing = jnp.zeros((1, COLS), jnp.float32)
    for b in range(n_lat):
        def below(blocks):
            return blocks(b - 1)[ROWS - 1 : ROWS] if b > 0 else nothing

        def above(blocks):
            return blocks(b + 1)[0:1] if b + 1 < n_lat else nothing

        merid = combined[b, 3]
        for f in range(3):
            out_ref[b, f * ROWS : (f + 1) * ROWS, :] = combined[b, f]
        out_ref[b, 24:32, :] = row_below(merid, below(lambda i: combined[i, 3])) - row_above(
            merid, above(lambda i: combined[i, 3])
        )
        out_ref[b, 32:33, :] = below(lambda i: combined[i, 0])
        out_ref[b, 33:34, :] = above(lambda i: combined[i, 0])
        out_ref[b, 34:35, :] = below(lambda i: combined[i, 1])
        out_ref[b, 35:36, :] = above(lambda i: combined[i, 1])
        out_ref[b, 36:37, :] = below(lambda i: corners[i])
        out_ref[b, 37:38, :] = above(lambda i: corners[i])
        out_ref[b, 38:40, :] = jnp.zeros((2, COLS), jnp.float32)
        columns = jnp.zeros((ROWS, COLS), jnp.float32)
        for f in range(3):
            moved = pltpu.roll(beyond[f], (COLS + 2 * f - 2 * b) % COLS, 1)
            columns = jnp.where((lanes >= 2 * f) & (lanes < 2 * f + 2), moved, columns)
        out_ref[b, 40:48, :] = columns


def assemble(combined, inside, across):
    return pl.pallas_call(
        assemble_kernel,
        out_shape=jax.ShapeDtypeStruct((combined.shape[0], SUM_ROWS, COLS), jnp.float32),
        in_specs=[VMEM_SPEC] * 3,
        out_specs=VMEM_SPEC,
        compiler_params=pltpu.CompilerParams(vmem_limit_bytes=SMALL),
        name="assemble_sends",
    )(in_vmem(combined), in_vmem(inside), in_vmem(across))


def backward_kernel(targets, gathered, inside, across, tiles_hbm, out_ref, zonal, merid, rows_ref, tiles, sems):
    n_lat = gathered.shape[0]
    tile_count = tiles.shape[0]
    copies = [
        pltpu.make_async_copy(tiles_hbm.at[k], tiles.at[k], sems.at[k]) for k in range(tile_count)
    ]
    for copy in copies:
        copy.start()
    lanes = lax.broadcasted_iota(jnp.int32, (ROWS, COLS), 1)
    nothing = jnp.zeros((1, COLS), jnp.float32)
    west_edges, east_edges = west_and_east(inside[3 * ROWS :, :], across[3 * ROWS :, :])
    for b in range(n_lat):
        here = gathered[b, ROWS : 2 * ROWS, :]
        shift = COLS - 1 - 2 * b
        eastern = jnp.where(
            lanes == COLS - 1, pltpu.roll(east_edges, shift, 1), pltpu.roll(here, COLS - 1, 1)
        )
        western = jnp.where(lanes == 0, pltpu.roll(west_edges, shift, 1), pltpu.roll(here, 1, 1))
        above = gathered[b + 1, ROWS : ROWS + 1, :] if b + 1 < n_lat else nothing
        below = gathered[b - 1, 2 * ROWS - 1 : 2 * ROWS, :] if b > 0 else nothing
        zonal[b] = -0.5 * (eastern - western)
        merid[b] = -0.5 * (row_above(here, above) - row_below(here, below))
    rows_ref[...] = jnp.zeros_like(rows_ref)
    for k in range(tile_count):
        target = targets[0, k]
        for row in range(ROWS):
            columns = slice(row * COLS, (row + 1) * COLS)
            rows_ref[k, 0:1, columns] = zonal[target, row : row + 1, :]
            rows_ref[k, 1:2, columns] = merid[target, row : row + 1, :]
    total = jnp.zeros((ROWS, tiles.shape[2]), jnp.float32)
    for k in range(tile_count):
        copies[k].wait()
        total += jnp.dot(
            rows_ref[k].astype(jnp.bfloat16), tiles[k], preferred_element_type=jnp.float32
        )
    out_ref[...] = total[0:2]


def backward(targets, gathered, inside, across, tiles):
    n_lat = gathered.shape[0]
    tile_count, mag_cells, geo_cells = tiles.shape
    return pl.pallas_call(
        backward_kernel,
        out_shape=jax.ShapeDtypeStruct((2, geo_cells), jnp.float32),
        in_specs=[SMEM_SPEC, VMEM_SPEC, VMEM_SPEC, VMEM_SPEC, HBM_SPEC],
        out_specs=VMEM_SPEC,
        scratch_shapes=[
            pltpu.VMEM((n_lat, ROWS, COLS), jnp.float32),
            pltpu.VMEM((n_lat, ROWS, COLS), jnp.float32),
            pltpu.VMEM((tile_count, ROWS, mag_cells), jnp.float32),
            pltpu.VMEM(tiles.shape, tiles.dtype),
            pltpu.SemaphoreType.DMA((tile_count,)),
        ],
        compiler_params=pltpu.CompilerParams(vmem_limit_bytes=SCOPED),
        cost_estimate=pl.CostEstimate(
            flops=16 * tiles.size, bytes_accessed=2 * tiles.size, transcendentals=0
        ),
        name="electric_to_geo",
    )(targets, in_vmem(gathered), in_vmem(inside), in_vmem(across), tiles)


def stencil_kernel(received, stencil_ref, source_ref):
    sums = received[0]
    for source in range(1, received.shape[0]):
        sums += received[source]
    lanes = lax.broadcasted_iota(jnp.int32, (ROWS, COLS), 1)
    columns = sums[40:48]

    def eastward(block, beyond, lane):
        moved = pltpu.roll(beyond, COLS - 1 - lane, 1)
        return jnp.where(lanes == COLS - 1, moved, pltpu.roll(block, COLS - 1, 1))

    def westward(block, beyond, lane):
        moved = pltpu.roll(beyond, (COLS - lane) % COLS, 1)
        return jnp.where(lanes == 0, moved, pltpu.roll(block, 1, 1))

    center0, center1, zonal, merid, edge = (sums[i * ROWS : (i + 1) * ROWS] for i in range(5))
    corner = pltpu.roll(edge, ROWS - 2, 0)
    edge_east, edge_west = eastward(edge, corner, 0), westward(edge, corner, 1)
    east1, west1 = eastward(center1, columns, 2), westward(center1, columns, 3)
    east_coef = 0.5 * (center0 + eastward(center0, columns, 0))
    west_coef = 0.5 * (center0 + westward(center0, columns, 1))
    north_coef = 0.5 * (center0 + row_above(center0, edge[1:2]))
    south_coef = 0.5 * (center0 + row_below(center0, edge[0:1]))
    ne_coef = 0.25 * (row_above(east1, edge_east[3:4]) - center1)
    nw_coef = -0.25 * (row_above(west1, edge_west[3:4]) - center1)
    se_coef = -0.25 * (row_below(east1, edge_east[2:3]) - center1)
    sw_coef = 0.25 * (row_below(west1, edge_west[2:3]) - center1)
    others = [east_coef, west_coef, north_coef, south_coef, ne_coef, nw_coef, se_coef, sw_coef]
    stencil_ref[0] = -sum(others[1:], others[0])
    for i, coef in enumerate(others):
        stencil_ref[i + 1] = coef
    source_ref[...] = (
        0.5 * (eastward(zonal, columns, 4) - westward(zonal, columns, 5)) + 0.5 * merid
    )


def stencil_source(received):
    return pl.pallas_call(
        stencil_kernel,
        out_shape=(
            jax.ShapeDtypeStruct((9, ROWS, COLS), jnp.float32),
            jax.ShapeDtypeStruct((ROWS, COLS), jnp.float32),
        ),
        in_specs=[VMEM_SPEC],
        out_specs=(VMEM_SPEC, VMEM_SPEC),
        compiler_params=pltpu.CompilerParams(vmem_limit_bytes=SMALL),
        name="stencil_source",
    )(in_vmem(received))


def lon_neighbours(block):
    count = lax.axis_size("lon")
    inside = [(i, i ^ 1) for i in range(count)]
    across = [(i, (i + 1 if i % 2 else i - 1) % count) for i in range(count)]
    return lax.ppermute(block, "lon", inside), lax.ppermute(block, "lon", across)


def west_and_east(inside, across):
    even = lax.axis_index("lon") % 2 == 0
    return jnp.where(even, across, inside), jnp.where(even, inside, across)


def per_device(
    conductivity, wind_terms, correlation_tiles, tile_targets, level_weights, line_levels, potential
):
    n_lat = lax.axis_size("lat")
    tiles = in_hbm(correlation_tiles)
    near_count = tiles.shape[0] // 2
    packed = pack(line_levels, potential, n_lat)
    gathered = lax.all_to_all(packed, "lat", 0, 0, tiled=True)
    near_plain, near_wind, far_plain, far_wind = product(in_hbm(conductivity), in_hbm(wind_terms), tiles, near_count)
    combined, edges = integral(tile_targets, level_weights, gathered, (near_plain, near_wind), (far_plain, far_wind))
    inside, across = lon_neighbours(edges)
    sends = assemble(combined, inside, across)
    received = lax.all_to_all(sends, "lat", 0, 0, tiled=True)
    geo_field = backward(tile_targets, gathered, inside, across, tiles)
    stencil, source_term = stencil_source(received)
    return stencil, source_term, geo_field


def solution(mesh):
    in_specs = (
        P(None, None, ("lat", "lon")),
        P(None, None, ("lat", "lon")),
        P(("lat", "lon"), None, None),
        P(("lat", "lon"), None),
        P(),
        P(None, "lat", "lon"),
        P("lat", "lon"),
    )
    out_specs = (P(None, "lat", "lon"), P("lat", "lon"), P(None, ("lat", "lon")))
    return jax.shard_map(
        per_device, mesh=mesh, in_specs=in_specs, out_specs=out_specs, check_vma=False
    )
```

```python
import functools

import jax
import jax.numpy as jnp
from jax import lax
from jax.experimental import pallas as pl
from jax.experimental.pallas import tpu as pltpu
from jax.sharding import PartitionSpec as P

RADIX = 128.0
ROWS, COLS = 8, 128
SUM_ROWS = 64
SCOPED = 24 * 2**20
SMALL = 8 * 2**20
CHUNK = 2 * COLS
VMEM_SPEC = pl.BlockSpec(memory_space=pltpu.VMEM)
HBM_SPEC = pl.BlockSpec(memory_space=pltpu.HBM)
SMEM_SPEC = pl.BlockSpec(memory_space=pltpu.SMEM)


def pack_kernel(levels_ref, potential_ref, out_ref):
    packed = levels_ref[0].astype(jnp.float32) * RADIX + levels_ref[1].astype(jnp.float32)
    potential = potential_ref[...]
    for target in range(out_ref.shape[0]):
        out_ref[target, 0:ROWS, :] = packed
        out_ref[target, ROWS : 2 * ROWS, :] = potential


def pack(line_levels, potential, n_lat):
    return pl.pallas_call(
        pack_kernel,
        out_shape=pltpu.VMEM((n_lat, 2 * ROWS, COLS), jnp.float32),
        in_specs=[VMEM_SPEC] * 2,
        out_specs=VMEM_SPEC,
        name="pack_levels_potential",
    )(line_levels, potential)


def row_above(block, edge):
    rows = lax.broadcasted_iota(jnp.int32, block.shape, 0)
    return jnp.where(rows == ROWS - 1, edge, pltpu.roll(block, ROWS - 1, 0))


def row_below(block, edge):
    rows = lax.broadcasted_iota(jnp.int32, block.shape, 0)
    return jnp.where(rows == 0, edge, pltpu.roll(block, 1, 0))


def in_vmem(array):
    return pltpu.with_memory_space_constraint(array, pltpu.VMEM)


def in_hbm(array):
    return pltpu.with_memory_space_constraint(array, pltpu.HBM)


def product_kernel(
    conductivity_hbm, wind_hbm, tiles_hbm, near_plain, near_wind, far_plain_hbm, far_wind_hbm,
    fields, conductivity, wind, tiles, far_plain, far_wind, sems, far_sems,
):
    tile_count, mag_cells, geo_cells = tiles.shape
    levels_n = conductivity.shape[1]
    near_count = near_plain.shape[0]
    order = list(range(near_count, tile_count)) + list(range(near_count))
    field_copies = [
        pltpu.make_async_copy(conductivity_hbm, conductivity, sems.at[tile_count]),
        pltpu.make_async_copy(wind_hbm, wind, sems.at[tile_count + 1]),
    ]
    def tile_copy(k):
        return pltpu.make_async_copy(tiles_hbm.at[k], tiles.at[k], sems.at[k])

    for copy in field_copies + [tile_copy(k) for k in order]:
        copy.start()
    for copy in field_copies:
        copy.wait()
    fields[0:levels_n, :] = conductivity[0]
    fields[levels_n : 2 * levels_n, :] = conductivity[1]
    first, second, third, fourth = (wind[i].astype(jnp.float32) for i in range(4))
    fields[2 * levels_n : 3 * levels_n, :] = (third - second).astype(jnp.bfloat16)
    fields[3 * levels_n : 4 * levels_n, :] = (first + fourth).astype(jnp.bfloat16)
    def multiply(k, plain_out, wind_out, i):
        tile_copy(k).wait()
        for start in range(0, mag_cells, CHUNK):
            columns = slice(start, start + CHUNK)
            value = lax.dot_general(
                fields[...],
                tiles[k, columns, :],
                (((1,), (1,)), ((), ())),
                preferred_element_type=jnp.float32,
            )
            plain_out[i, :, columns] = value[: 2 * levels_n].astype(jnp.bfloat16)
            wind_out[i, :, columns] = value[2 * levels_n :]

    def far_outputs(i):
        return (
            pltpu.make_async_copy(far_plain.at[i], far_plain_hbm.at[i], far_sems.at[2 * i]),
            pltpu.make_async_copy(far_wind.at[i], far_wind_hbm.at[i], far_sems.at[2 * i + 1]),
        )

    @pl.loop(0, tile_count - near_count)
    def _(i):
        multiply(near_count + i, far_plain, far_wind, i)
        for copy in far_outputs(i):
            copy.start()

    @pl.loop(0, near_count)
    def _(i):
        multiply(i, near_plain, near_wind, i)

    for i in range(tile_count - near_count):
        for copy in far_outputs(i):
            copy.wait()


def product(conductivity, wind, tiles, near_count):
    levels_n, geo_cells = conductivity.shape[1:]
    tile_count, mag_cells = tiles.shape[:2]
    far_count = tile_count - near_count
    near_shape, far_shape = ((count, 2 * levels_n, mag_cells) for count in (near_count, far_count))
    return pl.pallas_call(
        product_kernel,
        out_shape=(
            pltpu.VMEM(near_shape, jnp.bfloat16),
            pltpu.VMEM(near_shape, jnp.float32),
            pltpu.HBM(far_shape, jnp.bfloat16),
            pltpu.HBM(far_shape, jnp.float32),
        ),
        in_specs=[HBM_SPEC] * 3,
        out_specs=(VMEM_SPEC, VMEM_SPEC, HBM_SPEC, HBM_SPEC),
        scratch_shapes=[
            pltpu.VMEM((4 * levels_n, geo_cells), jnp.bfloat16),
            pltpu.VMEM(conductivity.shape, conductivity.dtype),
            pltpu.VMEM(wind.shape, wind.dtype),
            pltpu.VMEM(tiles.shape, tiles.dtype),
            pltpu.VMEM(far_shape, jnp.bfloat16),
            pltpu.VMEM(far_shape, jnp.float32),
            pltpu.SemaphoreType.DMA((tile_count + 2,)),
            pltpu.SemaphoreType.DMA((2 * far_count,)),
        ],
        compiler_params=pltpu.CompilerParams(vmem_limit_bytes=SCOPED),
        cost_estimate=pl.CostEstimate(
            flops=2 * 4 * levels_n * tiles.size, bytes_accessed=2 * tiles.size, transcendentals=0
        ),
        name="regrid_product",
    )(conductivity, wind, tiles)


def integral_kernel(
    targets, level_weights, gathered, near_plain, near_wind, far_plain_hbm, far_wind_hbm, combined, edges,
    weights, plain, mirrored, far_plain, far_wind, sems,
):
    near_count, far_count = near_plain.shape[0], far_plain.shape[0]
    levels_n = level_weights.shape[0]
    n_lat = gathered.shape[0]
    def far_inputs(i):
        return (
            pltpu.make_async_copy(far_plain_hbm.at[i], far_plain.at[i], sems.at[2 * i]),
            pltpu.make_async_copy(far_wind_hbm.at[i], far_wind.at[i], sems.at[2 * i + 1]),
        )

    for i in range(far_count):
        for copy in far_inputs(i):
            copy.start()
    for level in range(levels_n):
        weights[level : level + 1, :] = jnp.full((1, COLS), level_weights[level], jnp.float32)
    plain[...] = jnp.zeros_like(plain)
    mirrored[...] = jnp.zeros_like(mirrored)
    level_of = lax.broadcasted_iota(jnp.int32, (levels_n, COLS), 0).astype(jnp.float32)

    def integrate(k, plain_part, wind_part, i):
        target = targets[0, k]
        for row in range(ROWS):
            bounds = gathered[target, row : row + 1, :]
            low = jnp.floor(bounds * (1.0 / RADIX))
            high = bounds - low * RADIX
            inside = (level_of >= low) & (level_of < high)
            weight = jnp.where(inside, weights[...], 0.0)
            for f in range(4):
                planes = (plain_part, wind_part)[f // 2]
                rows = slice(f % 2 * levels_n, (f % 2 + 1) * levels_n)
                part = planes[i, rows, row * COLS : (row + 1) * COLS]
                total = jnp.sum(part.astype(jnp.float32) * weight, axis=0, keepdims=True)
                plain[target, f, row : row + 1, :] = total
                mirrored[n_lat - 1 - target, f, ROWS - 1 - row : ROWS - row, :] = total

    @pl.loop(0, near_count)
    def _(i):
        integrate(i, near_plain, near_wind, i)

    @pl.loop(0, far_count)
    def _(i):
        for copy in far_inputs(i):
            copy.wait()
        integrate(near_count + i, far_plain, far_wind, i)

    lanes = lax.broadcasted_iota(jnp.int32, (ROWS, COLS), 1)
    for f in range(4):
        for b in range(n_lat):
            combined[b, f] = plain[b, f] + mirrored[b, f]

    def both_edges(block_of):
        edge = jnp.zeros((ROWS, COLS), jnp.float32)
        for b in range(n_lat):
            block = block_of(b)
            edge = jnp.where(lanes == 2 * b, pltpu.roll(block, 2 * b, 1), edge)
            edge = jnp.where(lanes == 2 * b + 1, pltpu.roll(block, 2 * b + 2, 1), edge)
        return edge

    for f in range(3):
        edges[f * ROWS : (f + 1) * ROWS, :] = both_edges(lambda b: combined[b, f])
    edges[3 * ROWS : 4 * ROWS, :] = both_edges(lambda b: gathered[b, ROWS : 2 * ROWS, :])


def integral(targets, level_weights, gathered, near, far):
    far_shape = far[0].shape
    n_lat = gathered.shape[0]
    return pl.pallas_call(
        integral_kernel,
        out_shape=(
            pltpu.VMEM((n_lat, 4, ROWS, COLS), jnp.float32),
            pltpu.VMEM((4 * ROWS, COLS), jnp.float32),
        ),
        in_specs=[SMEM_SPEC] * 2 + [VMEM_SPEC] * 3 + [HBM_SPEC] * 2,
        out_specs=(VMEM_SPEC, VMEM_SPEC),
        scratch_shapes=[
            pltpu.VMEM((level_weights.shape[0], COLS), jnp.float32),
            pltpu.VMEM((n_lat, 4, ROWS, COLS), jnp.float32),
            pltpu.VMEM((n_lat, 4, ROWS, COLS), jnp.float32),
            pltpu.VMEM(far_shape, jnp.bfloat16),
            pltpu.VMEM(far_shape, jnp.float32),
            pltpu.SemaphoreType.DMA((2 * far_shape[0],)),
        ],
        compiler_params=pltpu.CompilerParams(vmem_limit_bytes=SCOPED),
        cost_estimate=pl.CostEstimate(
            flops=6 * near[0].size, bytes_accessed=16 * near[0].size, transcendentals=0
        ),
        name="level_integral",
    )(targets, level_weights, in_vmem(gathered), *map(in_vmem, near), *map(in_hbm, far))


def assemble_kernel(combined, inside, across, out_ref):
    n_lat = combined.shape[0]
    lanes = lax.broadcasted_iota(jnp.int32, (ROWS, COLS), 1)
    beyond = []
    for f in range(3):
        rows = slice(f * ROWS, (f + 1) * ROWS)
        west, east = west_and_east(inside[rows, :], across[rows, :])
        beyond.append(jnp.where(lanes % 2 == 0, east, west))
    corners = [pltpu.roll(beyond[1], (COLS - 2 * b) % COLS, 1) for b in range(n_lat)]
    nothing = jnp.zeros((1, COLS), jnp.float32)
    for b in range(n_lat):
        def below(blocks):
            return blocks(b - 1)[ROWS - 1 : ROWS] if b > 0 else nothing

        def above(blocks):
            return blocks(b + 1)[0:1] if b + 1 < n_lat else nothing

        merid = row_below(combined[b, 3], below(lambda i: combined[i, 3])) - row_above(
            combined[b, 3], above(lambda i: combined[i, 3])
        )
        outside = [
            below(lambda i: combined[i, 0]),
            above(lambda i: combined[i, 0]),
            below(lambda i: combined[i, 1]),
            above(lambda i: combined[i, 1]),
            below(lambda i: corners[i]),
            above(lambda i: corners[i]),
            nothing,
            nothing,
        ]
        columns = jnp.zeros((ROWS, COLS), jnp.float32)
        for f in range(3):
            moved = pltpu.roll(beyond[f], (COLS + 2 * f - 2 * b) % COLS, 1)
            columns = jnp.where((lanes >= 2 * f) & (lanes < 2 * f + 2), moved, columns)

        def put(start, *blocks):
            out_ref[b, start : start + 2 * ROWS, :] = jnp.concatenate(blocks, 0).astype(jnp.bfloat16)

        put(0, combined[b, 0], combined[b, 1])
        put(16, *both_parts(combined[b, 2]))
        put(32, *both_parts(merid))
        put(48, *outside, columns)


def both_parts(block):
    first = block.astype(jnp.bfloat16).astype(jnp.float32)
    return first, block - first


def assemble(combined, inside, across):
    return pl.pallas_call(
        assemble_kernel,
        out_shape=jax.ShapeDtypeStruct((combined.shape[0], SUM_ROWS, COLS), jnp.bfloat16),
        in_specs=[VMEM_SPEC] * 3,
        out_specs=VMEM_SPEC,
        compiler_params=pltpu.CompilerParams(vmem_limit_bytes=SMALL),
        name="assemble_sends",
    )(in_vmem(combined), in_vmem(inside), in_vmem(across))


def backward_kernel(targets, gathered, inside, across, tiles_hbm, out_ref, zonal, merid, rows_ref, tiles, sems):
    n_lat = gathered.shape[0]
    tile_count = tiles.shape[0]
    copies = [
        pltpu.make_async_copy(tiles_hbm.at[k], tiles.at[k], sems.at[k]) for k in range(tile_count)
    ]
    for copy in copies:
        copy.start()
    lanes = lax.broadcasted_iota(jnp.int32, (ROWS, COLS), 1)
    nothing = jnp.zeros((1, COLS), jnp.float32)
    west_edges, east_edges = west_and_east(inside[3 * ROWS :, :], across[3 * ROWS :, :])
    for b in range(n_lat):
        here = gathered[b, ROWS : 2 * ROWS, :]
        shift = COLS - 1 - 2 * b
        eastern = jnp.where(
            lanes == COLS - 1, pltpu.roll(east_edges, shift, 1), pltpu.roll(here, COLS - 1, 1)
        )
        western = jnp.where(lanes == 0, pltpu.roll(west_edges, shift, 1), pltpu.roll(here, 1, 1))
        above = gathered[b + 1, ROWS : ROWS + 1, :] if b + 1 < n_lat else nothing
        below = gathered[b - 1, 2 * ROWS - 1 : 2 * ROWS, :] if b > 0 else nothing
        zonal[b] = -0.5 * (eastern - western)
        merid[b] = -0.5 * (row_above(here, above) - row_below(here, below))
    rows_ref[...] = jnp.zeros_like(rows_ref)
    for k in range(tile_count):
        target = targets[0, k]
        for row in range(ROWS):
            columns = slice(row * COLS, (row + 1) * COLS)
            rows_ref[k, 0:1, columns] = zonal[target, row : row + 1, :]
            rows_ref[k, 1:2, columns] = merid[target, row : row + 1, :]
    total = jnp.zeros((ROWS, tiles.shape[2]), jnp.float32)
    for k in range(tile_count):
        copies[k].wait()
        total += jnp.dot(
            rows_ref[k].astype(jnp.bfloat16), tiles[k], preferred_element_type=jnp.float32
        )
    out_ref[...] = total[0:2]


def backward(targets, gathered, inside, across, tiles):
    n_lat = gathered.shape[0]
    tile_count, mag_cells, geo_cells = tiles.shape
    return pl.pallas_call(
        backward_kernel,
        out_shape=jax.ShapeDtypeStruct((2, geo_cells), jnp.float32),
        in_specs=[SMEM_SPEC, VMEM_SPEC, VMEM_SPEC, VMEM_SPEC, HBM_SPEC],
        out_specs=VMEM_SPEC,
        scratch_shapes=[
            pltpu.VMEM((n_lat, ROWS, COLS), jnp.float32),
            pltpu.VMEM((n_lat, ROWS, COLS), jnp.float32),
            pltpu.VMEM((tile_count, ROWS, mag_cells), jnp.float32),
            pltpu.VMEM(tiles.shape, tiles.dtype),
            pltpu.SemaphoreType.DMA((tile_count,)),
        ],
        compiler_params=pltpu.CompilerParams(vmem_limit_bytes=SCOPED),
        cost_estimate=pl.CostEstimate(
            flops=16 * tiles.size, bytes_accessed=2 * tiles.size, transcendentals=0
        ),
        name="electric_to_geo",
    )(targets, in_vmem(gathered), in_vmem(inside), in_vmem(across), tiles)


def stencil_kernel(received, stencil_ref, source_ref):
    sums = received[0].astype(jnp.float32)
    for source in range(1, received.shape[0]):
        sums += received[source].astype(jnp.float32)
    lanes = lax.broadcasted_iota(jnp.int32, (ROWS, COLS), 1)

    def eastward(block, beyond, lane):
        moved = pltpu.roll(beyond, COLS - 1 - lane, 1)
        return jnp.where(lanes == COLS - 1, moved, pltpu.roll(block, COLS - 1, 1))

    def westward(block, beyond, lane):
        moved = pltpu.roll(beyond, (COLS - lane) % COLS, 1)
        return jnp.where(lanes == 0, moved, pltpu.roll(block, 1, 1))

    center0, center1, zonal, zonal_left, merid, merid_left, edge, columns = (
        sums[i * ROWS : (i + 1) * ROWS] for i in range(8)
    )
    zonal, merid = zonal + zonal_left, merid + merid_left
    corner = pltpu.roll(edge, ROWS - 2, 0)
    edge_east, edge_west = eastward(edge, corner, 0), westward(edge, corner, 1)
    east1, west1 = eastward(center1, columns, 2), westward(center1, columns, 3)
    east_coef = 0.5 * (center0 + eastward(center0, columns, 0))
    west_coef = 0.5 * (center0 + westward(center0, columns, 1))
    north_coef = 0.5 * (center0 + row_above(center0, edge[1:2]))
    south_coef = 0.5 * (center0 + row_below(center0, edge[0:1]))
    ne_coef = 0.25 * (row_above(east1, edge_east[3:4]) - center1)
    nw_coef = -0.25 * (row_above(west1, edge_west[3:4]) - center1)
    se_coef = -0.25 * (row_below(east1, edge_east[2:3]) - center1)
    sw_coef = 0.25 * (row_below(west1, edge_west[2:3]) - center1)
    others = [east_coef, west_coef, north_coef, south_coef, ne_coef, nw_coef, se_coef, sw_coef]
    stencil_ref[0] = -sum(others[1:], others[0])
    for i, coef in enumerate(others):
        stencil_ref[i + 1] = coef
    source_ref[...] = (
        0.5 * (eastward(zonal, columns, 4) - westward(zonal, columns, 5)) + 0.5 * merid
    )


def stencil_source(received):
    return pl.pallas_call(
        stencil_kernel,
        out_shape=(
            jax.ShapeDtypeStruct((9, ROWS, COLS), jnp.float32),
            jax.ShapeDtypeStruct((ROWS, COLS), jnp.float32),
        ),
        in_specs=[VMEM_SPEC],
        out_specs=(VMEM_SPEC, VMEM_SPEC),
        compiler_params=pltpu.CompilerParams(vmem_limit_bytes=SMALL),
        name="stencil_source",
    )(in_vmem(received))


def lon_neighbours(block):
    count = lax.axis_size("lon")
    inside = [(i, i ^ 1) for i in range(count)]
    across = [(i, (i + 1 if i % 2 else i - 1) % count) for i in range(count)]
    return lax.ppermute(block, "lon", inside), lax.ppermute(block, "lon", across)


def west_and_east(inside, across):
    even = lax.axis_index("lon") % 2 == 0
    return jnp.where(even, across, inside), jnp.where(even, inside, across)


def per_device(
    conductivity, wind_terms, correlation_tiles, tile_targets, level_weights, line_levels, potential
):
    n_lat = lax.axis_size("lat")
    tiles = in_hbm(correlation_tiles)
    near_count = tiles.shape[0] // 2
    packed = pack(line_levels, potential, n_lat)
    gathered = lax.all_to_all(packed, "lat", 0, 0, tiled=True)
    near_plain, near_wind, far_plain, far_wind = product(in_hbm(conductivity), in_hbm(wind_terms), tiles, near_count)
    combined, edges = integral(tile_targets, level_weights, gathered, (near_plain, near_wind), (far_plain, far_wind))
    inside, across = lon_neighbours(edges)
    sends = assemble(combined, inside, across)
    received = lax.all_to_all(sends, "lat", 0, 0, tiled=True)
    geo_field = backward(tile_targets, gathered, inside, across, tiles)
    stencil, source_term = stencil_source(received)
    return stencil, source_term, geo_field


def solution(mesh):
    in_specs = (
        P(None, None, ("lat", "lon")),
        P(None, None, ("lat", "lon")),
        P(("lat", "lon"), None, None),
        P(("lat", "lon"), None),
        P(),
        P(None, "lat", "lon"),
        P("lat", "lon"),
    )
    out_specs = (P(None, "lat", "lon"), P("lat", "lon"), P(None, ("lat", "lon")))
    return jax.shard_map(
        per_device, mesh=mesh, in_specs=in_specs, out_specs=out_specs, check_vma=False
    )
```

```python
import functools

import jax
import jax.numpy as jnp
from jax import lax
from jax.experimental import pallas as pl
from jax.experimental.pallas import tpu as pltpu
from jax.sharding import PartitionSpec as P

RADIX = 128.0
ROWS, COLS = 8, 128
SUM_ROWS = 64
SCOPED = 24 * 2**20
SMALL = 8 * 2**20
CHUNK = 2 * COLS
FAR_TILES = 2
VMEM_SPEC = pl.BlockSpec(memory_space=pltpu.VMEM)
HBM_SPEC = pl.BlockSpec(memory_space=pltpu.HBM)
SMEM_SPEC = pl.BlockSpec(memory_space=pltpu.SMEM)


def pack_kernel(levels_ref, potential_ref, out_ref):
    packed = levels_ref[0].astype(jnp.float32) * RADIX + levels_ref[1].astype(jnp.float32)
    potential = potential_ref[...]
    for target in range(out_ref.shape[0]):
        out_ref[target, 0:ROWS, :] = packed
        out_ref[target, ROWS : 2 * ROWS, :] = potential


def pack(line_levels, potential, n_lat):
    return pl.pallas_call(
        pack_kernel,
        out_shape=pltpu.VMEM((n_lat, 2 * ROWS, COLS), jnp.float32),
        in_specs=[VMEM_SPEC] * 2,
        out_specs=VMEM_SPEC,
        name="pack_levels_potential",
    )(line_levels, potential)


def row_above(block, edge):
    rows = lax.broadcasted_iota(jnp.int32, block.shape, 0)
    return jnp.where(rows == ROWS - 1, edge, pltpu.roll(block, ROWS - 1, 0))


def row_below(block, edge):
    rows = lax.broadcasted_iota(jnp.int32, block.shape, 0)
    return jnp.where(rows == 0, edge, pltpu.roll(block, 1, 0))


def in_vmem(array):
    return pltpu.with_memory_space_constraint(array, pltpu.VMEM)


def in_smem(array):
    return pltpu.with_memory_space_constraint(array, pltpu.SMEM)


def in_hbm(array):
    return pltpu.with_memory_space_constraint(array, pltpu.HBM)


def product_kernel(
    conductivity_hbm, wind_hbm, tiles_hbm, near_plain, near_zonal, near_merid, far_plain_hbm, far_zonal_hbm, far_merid_hbm,
    fields, conductivity, wind, tiles, far_plain, far_zonal, far_merid, sems, far_sems,
):
    tile_count, mag_cells, geo_cells = tiles.shape
    levels_n = conductivity.shape[1]
    near_count = near_plain.shape[0]
    order = list(range(near_count, tile_count)) + list(range(near_count))
    far_merid_count = far_merid.shape[0]
    field_copies = [
        pltpu.make_async_copy(conductivity_hbm, conductivity, sems.at[tile_count]),
        pltpu.make_async_copy(wind_hbm, wind, sems.at[tile_count + 1]),
    ]
    tile_copies = {
        k: pltpu.make_async_copy(tiles_hbm.at[k], tiles.at[k], sems.at[k]) for k in order
    }
    for copy in field_copies + [tile_copies[k] for k in order]:
        copy.start()
    for copy in field_copies:
        copy.wait()
    fields[0:levels_n, :] = conductivity[0]
    fields[levels_n : 2 * levels_n, :] = conductivity[1]
    first, second, third, fourth = (wind[i].astype(jnp.float32) for i in range(4))
    fields[2 * levels_n : 3 * levels_n, :] = (third - second).astype(jnp.bfloat16)
    fields[3 * levels_n : 4 * levels_n, :] = (first + fourth).astype(jnp.bfloat16)
    outputs = []

    def send(source, target):
        copy = pltpu.make_async_copy(source, target, far_sems.at[len(outputs)])
        copy.start()
        outputs.append(copy)

    for step, k in enumerate(order):
        tile_copies[k].wait()
        near, i = k < near_count, k if k < near_count else k - near_count
        plain_out, zonal_out = (near_plain, near_zonal) if near else (far_plain, far_zonal)
        merid_out, m = (far_merid, step) if step < far_merid_count else (near_merid, step - far_merid_count)
        for start in range(0, mag_cells, CHUNK):
            columns = slice(start, start + CHUNK)
            value = lax.dot_general(
                fields[...],
                tiles[k, columns, :],
                (((1,), (1,)), ((), ())),
                preferred_element_type=jnp.float32,
            )
            plain_out[i, :, columns] = value[: 2 * levels_n].astype(jnp.bfloat16)
            zonal_out[i, :, columns] = value[2 * levels_n : 3 * levels_n]
            merid_out[m, :, columns] = value[3 * levels_n :]
        if not near:
            send(far_plain.at[i], far_plain_hbm.at[i])
            send(far_zonal.at[i], far_zonal_hbm.at[i])
        if step < far_merid_count:
            send(far_merid.at[m], far_merid_hbm.at[m])
    for copy in outputs:
        copy.wait()


def product(conductivity, wind, tiles, near_count):
    levels_n, geo_cells = conductivity.shape[1:]
    tile_count, mag_cells = tiles.shape[:2]
    far_count = tile_count - near_count
    plain = lambda count: ((count, 2 * levels_n, mag_cells), jnp.bfloat16)
    wind_term = lambda count: ((count, levels_n, mag_cells), jnp.float32)
    return pl.pallas_call(
        product_kernel,
        out_shape=(
            pltpu.VMEM(*plain(near_count)),
            pltpu.VMEM(*wind_term(near_count)),
            pltpu.VMEM(*wind_term(1)),
            pltpu.HBM(*plain(far_count)),
            pltpu.HBM(*wind_term(far_count)),
            pltpu.HBM(*wind_term(tile_count - 1)),
        ),
        in_specs=[HBM_SPEC] * 3,
        out_specs=(VMEM_SPEC,) * 3 + (HBM_SPEC,) * 3,
        scratch_shapes=[
            pltpu.VMEM((4 * levels_n, geo_cells), jnp.bfloat16),
            pltpu.VMEM(conductivity.shape, conductivity.dtype),
            pltpu.VMEM(wind.shape, wind.dtype),
            pltpu.VMEM(tiles.shape, tiles.dtype),
            pltpu.VMEM(*plain(far_count)),
            pltpu.VMEM(*wind_term(far_count)),
            pltpu.VMEM(*wind_term(tile_count - 1)),
            pltpu.SemaphoreType.DMA((tile_count + 2,)),
            pltpu.SemaphoreType.DMA((2 * far_count + tile_count - 1,)),
        ],
        compiler_params=pltpu.CompilerParams(vmem_limit_bytes=SCOPED),
        cost_estimate=pl.CostEstimate(
            flops=2 * 4 * levels_n * tiles.size, bytes_accessed=2 * tiles.size, transcendentals=0
        ),
        name="regrid_product",
    )(conductivity, wind, tiles)


def masked_weights(target, row, gathered, weights):
    levels_n = weights.shape[0]
    level_of = lax.broadcasted_iota(jnp.int32, (levels_n, COLS), 0).astype(jnp.float32)
    bounds = gathered[target, row : row + 1, :]
    low = jnp.floor(bounds * (1.0 / RADIX))
    high = bounds - low * RADIX
    inside = (level_of >= low) & (level_of < high)
    return jnp.where(inside, weights[...], 0.0)


def fill_weights(level_weights, weights):
    for level in range(weights.shape[0]):
        weights[level : level + 1, :] = jnp.full((1, COLS), level_weights[level], jnp.float32)


def integral_kernel(
    targets, level_weights, gathered, near_plain, near_zonal, far_plain_hbm, far_zonal_hbm, combined, edges,
    weights, plain, mirrored, far_plain, far_zonal, sems,
):
    near_count, far_count = near_plain.shape[0], far_plain.shape[0]
    levels_n = level_weights.shape[0]
    n_lat = gathered.shape[0]

    def far_inputs(i):
        return (
            pltpu.make_async_copy(far_plain_hbm.at[i], far_plain.at[i], sems.at[2 * i]),
            pltpu.make_async_copy(far_zonal_hbm.at[i], far_zonal.at[i], sems.at[2 * i + 1]),
        )

    for i in range(far_count):
        for copy in far_inputs(i):
            copy.start()
    fill_weights(level_weights, weights)
    plain[...] = jnp.zeros_like(plain)
    mirrored[...] = jnp.zeros_like(mirrored)

    def integrate(k, plain_part, zonal_part, i):
        target = targets[0, k]
        opposite = n_lat - 1 - target
        for row in range(ROWS):
            columns = slice(row * COLS, (row + 1) * COLS)
            weight = masked_weights(target, row, gathered, weights)
            for f in range(3):
                planes = zonal_part if f == 2 else plain_part
                start = 0 if f == 2 else f * levels_n
                part = planes[i, start : start + levels_n, columns]
                total = jnp.sum(part.astype(jnp.float32) * weight, axis=0, keepdims=True)
                plain[target, f * ROWS + row : f * ROWS + row + 1, :] = total
                last = (f + 1) * ROWS - 1 - row
                mirrored[opposite, last : last + 1, :] = total

    @pl.loop(0, near_count)
    def _(i):
        integrate(i, near_plain, near_zonal, i)

    @pl.loop(0, far_count)
    def _(i):
        for copy in far_inputs(i):
            copy.wait()
        integrate(near_count + i, far_plain, far_zonal, i)

    lanes = lax.broadcasted_iota(jnp.int32, (ROWS, COLS), 1)
    for b in range(n_lat):
        combined[b] = plain[b] + mirrored[b]

    def both_edges(block_of):
        edge = jnp.zeros((ROWS, COLS), jnp.float32)
        for b in range(n_lat):
            block = block_of(b)
            edge = jnp.where(lanes == 2 * b, pltpu.roll(block, 2 * b, 1), edge)
            edge = jnp.where(lanes == 2 * b + 1, pltpu.roll(block, 2 * b + 2, 1), edge)
        return edge

    for f in range(3):
        rows = slice(f * ROWS, (f + 1) * ROWS)
        edges[rows, :] = both_edges(lambda b: combined[b, rows, :])
    edges[3 * ROWS : 4 * ROWS, :] = both_edges(lambda b: gathered[b, ROWS : 2 * ROWS, :])


def integral(targets, level_weights, gathered, near, far):
    far_count = far[0].shape[0]
    levels_n = level_weights.shape[0]
    n_lat = gathered.shape[0]
    return pl.pallas_call(
        integral_kernel,
        out_shape=(
            pltpu.VMEM((n_lat, 3 * ROWS, COLS), jnp.float32),
            pltpu.VMEM((4 * ROWS, COLS), jnp.float32),
        ),
        in_specs=[SMEM_SPEC] * 2 + [VMEM_SPEC] * 3 + [HBM_SPEC] * 2,
        out_specs=(VMEM_SPEC, VMEM_SPEC),
        scratch_shapes=[
            pltpu.VMEM((levels_n, COLS), jnp.float32),
            pltpu.VMEM((n_lat, 3 * ROWS, COLS), jnp.float32),
            pltpu.VMEM((n_lat, 3 * ROWS, COLS), jnp.float32),
            pltpu.VMEM(far[0].shape, far[0].dtype),
            pltpu.VMEM(far[1].shape, far[1].dtype),
            pltpu.SemaphoreType.DMA((2 * far_count,)),
        ],
        compiler_params=pltpu.CompilerParams(vmem_limit_bytes=SCOPED),
        cost_estimate=pl.CostEstimate(
            flops=6 * near[0].size, bytes_accessed=16 * near[0].size, transcendentals=0
        ),
        name="level_integral",
    )(in_smem(targets), in_smem(level_weights), in_vmem(gathered), *map(in_vmem, near), *map(in_hbm, far))


def meridional_kernel(
    targets, level_weights, gathered, near, far_hbm, out_ref, weights, total, far, sems
):
    far_count = far.shape[0]
    tile_count = targets.shape[1]
    levels_n = level_weights.shape[0]
    n_lat = gathered.shape[0]
    shift = tile_count - FAR_TILES

    def far_input(i):
        return pltpu.make_async_copy(far_hbm.at[i], far.at[i], sems.at[i])

    for i in range(far_count):
        far_input(i).start()
    fill_weights(level_weights, weights)
    total[...] = jnp.zeros_like(total)

    def integrate(step, planes, i):
        target = targets[0, lax.rem(step + shift, tile_count)]
        for row in range(ROWS):
            columns = slice(row * COLS, (row + 1) * COLS)
            weight = masked_weights(target, row, gathered, weights)
            value = jnp.sum(planes[i, :, columns] * weight, axis=0, keepdims=True)
            total[0, target, row : row + 1, :] = value
            total[1, n_lat - 1 - target, ROWS - 1 - row : ROWS - row, :] = value

    integrate(far_count, near, 0)

    @pl.loop(0, far_count)
    def _(i):
        far_input(i).wait()
        integrate(i, far, i)

    merid = [total[0, b] + total[1, b] for b in range(n_lat)]
    nothing = jnp.zeros((1, COLS), jnp.float32)
    for b in range(n_lat):
        below = merid[b - 1][ROWS - 1 : ROWS] if b > 0 else nothing
        above = merid[b + 1][0:1] if b + 1 < n_lat else nothing
        out_ref[b] = row_below(merid[b], below) - row_above(merid[b], above)


def meridional(targets, level_weights, gathered, near, far):
    n_lat = gathered.shape[0]
    levels_n = level_weights.shape[0]
    return pl.pallas_call(
        meridional_kernel,
        out_shape=pltpu.VMEM((n_lat, ROWS, COLS), jnp.float32),
        in_specs=[SMEM_SPEC] * 2 + [VMEM_SPEC] * 2 + [HBM_SPEC],
        out_specs=VMEM_SPEC,
        scratch_shapes=[
            pltpu.VMEM((levels_n, COLS), jnp.float32),
            pltpu.VMEM((2, n_lat, ROWS, COLS), jnp.float32),
            pltpu.VMEM(far.shape, far.dtype),
            pltpu.SemaphoreType.DMA((far.shape[0],)),
        ],
        compiler_params=pltpu.CompilerParams(vmem_limit_bytes=SCOPED),
        cost_estimate=pl.CostEstimate(
            flops=4 * far.size, bytes_accessed=8 * far.size, transcendentals=0
        ),
        name="meridional_integral",
    )(in_smem(targets), in_smem(level_weights), in_vmem(gathered), in_vmem(near), in_hbm(far))


def assemble_kernel(combined, merid, inside, across, out_ref):
    n_lat = combined.shape[0]
    lanes = lax.broadcasted_iota(jnp.int32, (ROWS, COLS), 1)
    beyond = []
    for f in range(3):
        rows = slice(f * ROWS, (f + 1) * ROWS)
        west, east = west_and_east(inside[rows, :], across[rows, :])
        beyond.append(jnp.where(lanes % 2 == 0, east, west))
    corners = [pltpu.roll(beyond[1], (COLS - 2 * b) % COLS, 1) for b in range(n_lat)]
    nothing = jnp.zeros((1, COLS), jnp.float32)
    for b in range(n_lat):
        def below(blocks):
            return blocks(b - 1)[ROWS - 1 : ROWS] if b > 0 else nothing

        def above(blocks):
            return blocks(b + 1)[0:1] if b + 1 < n_lat else nothing

        outside = [
            below(lambda i: combined[i, 0:8]),
            above(lambda i: combined[i, 0:8]),
            below(lambda i: combined[i, 8:16]),
            above(lambda i: combined[i, 8:16]),
            below(lambda i: corners[i]),
            above(lambda i: corners[i]),
            nothing,
            nothing,
        ]
        columns = jnp.zeros((ROWS, COLS), jnp.float32)
        for f in range(3):
            moved = pltpu.roll(beyond[f], (COLS + 2 * f - 2 * b) % COLS, 1)
            columns = jnp.where((lanes >= 2 * f) & (lanes < 2 * f + 2), moved, columns)

        def put(start, *blocks):
            out_ref[b, start : start + 2 * ROWS, :] = jnp.concatenate(blocks, 0).astype(jnp.bfloat16)

        put(0, combined[b, 0:8], combined[b, 8:16])
        put(16, *both_parts(combined[b, 16:24]))
        put(32, *both_parts(merid[b]))
        put(48, *outside, columns)


def both_parts(block):
    first = block.astype(jnp.bfloat16).astype(jnp.float32)
    return first, block - first


def assemble(combined, merid, inside, across):
    return pl.pallas_call(
        assemble_kernel,
        out_shape=jax.ShapeDtypeStruct((combined.shape[0], SUM_ROWS, COLS), jnp.bfloat16),
        in_specs=[VMEM_SPEC] * 4,
        out_specs=VMEM_SPEC,
        compiler_params=pltpu.CompilerParams(vmem_limit_bytes=SMALL),
        name="assemble_sends",
    )(in_vmem(combined), in_vmem(merid), in_vmem(inside), in_vmem(across))


def backward_kernel(targets, gathered, inside, across, tiles_hbm, out_ref, zonal, merid, rows_ref, tiles, sems):
    n_lat = gathered.shape[0]
    tile_count = tiles.shape[0]
    copies = [
        pltpu.make_async_copy(tiles_hbm.at[k], tiles.at[k], sems.at[k]) for k in range(tile_count)
    ]
    for copy in copies:
        copy.start()
    lanes = lax.broadcasted_iota(jnp.int32, (ROWS, COLS), 1)
    nothing = jnp.zeros((1, COLS), jnp.float32)
    west_edges, east_edges = west_and_east(inside[3 * ROWS :, :], across[3 * ROWS :, :])
    for b in range(n_lat):
        here = gathered[b, ROWS : 2 * ROWS, :]
        shift = COLS - 1 - 2 * b
        eastern = jnp.where(
            lanes == COLS - 1, pltpu.roll(east_edges, shift, 1), pltpu.roll(here, COLS - 1, 1)
        )
        western = jnp.where(lanes == 0, pltpu.roll(west_edges, shift, 1), pltpu.roll(here, 1, 1))
        above = gathered[b + 1, ROWS : ROWS + 1, :] if b + 1 < n_lat else nothing
        below = gathered[b - 1, 2 * ROWS - 1 : 2 * ROWS, :] if b > 0 else nothing
        zonal[b] = -0.5 * (eastern - western)
        merid[b] = -0.5 * (row_above(here, above) - row_below(here, below))
    rows_ref[...] = jnp.zeros_like(rows_ref)
    for k in range(tile_count):
        target = targets[0, k]
        for row in range(ROWS):
            columns = slice(row * COLS, (row + 1) * COLS)
            rows_ref[k, 0:1, columns] = zonal[target, row : row + 1, :]
            rows_ref[k, 1:2, columns] = merid[target, row : row + 1, :]
    total = jnp.zeros((ROWS, tiles.shape[2]), jnp.float32)
    for k in range(tile_count):
        copies[k].wait()
        total += jnp.dot(
            rows_ref[k].astype(jnp.bfloat16), tiles[k], preferred_element_type=jnp.float32
        )
    out_ref[...] = total[0:2]


def backward(targets, gathered, inside, across, tiles):
    n_lat = gathered.shape[0]
    tile_count, mag_cells, geo_cells = tiles.shape
    return pl.pallas_call(
        backward_kernel,
        out_shape=jax.ShapeDtypeStruct((2, geo_cells), jnp.float32),
        in_specs=[SMEM_SPEC, VMEM_SPEC, VMEM_SPEC, VMEM_SPEC, HBM_SPEC],
        out_specs=VMEM_SPEC,
        scratch_shapes=[
            pltpu.VMEM((n_lat, ROWS, COLS), jnp.float32),
            pltpu.VMEM((n_lat, ROWS, COLS), jnp.float32),
            pltpu.VMEM((tile_count, ROWS, mag_cells), jnp.float32),
            pltpu.VMEM(tiles.shape, tiles.dtype),
            pltpu.SemaphoreType.DMA((tile_count,)),
        ],
        compiler_params=pltpu.CompilerParams(vmem_limit_bytes=SCOPED),
        cost_estimate=pl.CostEstimate(
            flops=16 * tiles.size, bytes_accessed=2 * tiles.size, transcendentals=0
        ),
        name="electric_to_geo",
    )(in_smem(targets), in_vmem(gathered), in_vmem(inside), in_vmem(across), tiles)


def stencil_kernel(received, stencil_ref, source_ref):
    sums = received[0].astype(jnp.float32)
    for source in range(1, received.shape[0]):
        sums += received[source].astype(jnp.float32)
    lanes = lax.broadcasted_iota(jnp.int32, (ROWS, COLS), 1)

    def eastward(block, beyond, lane):
        moved = pltpu.roll(beyond, COLS - 1 - lane, 1)
        return jnp.where(lanes == COLS - 1, moved, pltpu.roll(block, COLS - 1, 1))

    def westward(block, beyond, lane):
        moved = pltpu.roll(beyond, (COLS - lane) % COLS, 1)
        return jnp.where(lanes == 0, moved, pltpu.roll(block, 1, 1))

    center0, center1, zonal, zonal_left, merid, merid_left, edge, columns = (
        sums[i * ROWS : (i + 1) * ROWS] for i in range(8)
    )
    zonal, merid = zonal + zonal_left, merid + merid_left
    corner = pltpu.roll(edge, ROWS - 2, 0)
    edge_east, edge_west = eastward(edge, corner, 0), westward(edge, corner, 1)
    east1, west1 = eastward(center1, columns, 2), westward(center1, columns, 3)
    east_coef = 0.5 * (center0 + eastward(center0, columns, 0))
    west_coef = 0.5 * (center0 + westward(center0, columns, 1))
    north_coef = 0.5 * (center0 + row_above(center0, edge[1:2]))
    south_coef = 0.5 * (center0 + row_below(center0, edge[0:1]))
    ne_coef = 0.25 * (row_above(east1, edge_east[3:4]) - center1)
    nw_coef = -0.25 * (row_above(west1, edge_west[3:4]) - center1)
    se_coef = -0.25 * (row_below(east1, edge_east[2:3]) - center1)
    sw_coef = 0.25 * (row_below(west1, edge_west[2:3]) - center1)
    others = [east_coef, west_coef, north_coef, south_coef, ne_coef, nw_coef, se_coef, sw_coef]
    stencil_ref[0] = -sum(others[1:], others[0])
    for i, coef in enumerate(others):
        stencil_ref[i + 1] = coef
    source_ref[...] = (
        0.5 * (eastward(zonal, columns, 4) - westward(zonal, columns, 5)) + 0.5 * merid
    )


def stencil_source(received):
    return pl.pallas_call(
        stencil_kernel,
        out_shape=(
            jax.ShapeDtypeStruct((9, ROWS, COLS), jnp.float32),
            jax.ShapeDtypeStruct((ROWS, COLS), jnp.float32),
        ),
        in_specs=[VMEM_SPEC],
        out_specs=(VMEM_SPEC, VMEM_SPEC),
        compiler_params=pltpu.CompilerParams(vmem_limit_bytes=SMALL),
        name="stencil_source",
    )(in_vmem(received))


def lon_neighbours(block):
    count = lax.axis_size("lon")
    inside = [(i, i ^ 1) for i in range(count)]
    across = [(i, (i + 1 if i % 2 else i - 1) % count) for i in range(count)]
    return lax.ppermute(block, "lon", inside), lax.ppermute(block, "lon", across)


def west_and_east(inside, across):
    even = lax.axis_index("lon") % 2 == 0
    return jnp.where(even, across, inside), jnp.where(even, inside, across)


def per_device(
    conductivity, wind_terms, correlation_tiles, tile_targets, level_weights, line_levels, potential
):
    n_lat = lax.axis_size("lat")
    tiles = in_hbm(correlation_tiles)
    packed = pack(line_levels, potential, n_lat)
    gathered = lax.all_to_all(packed, "lat", 0, 0, tiled=True)
    near_plain, near_zonal, near_merid, far_plain, far_zonal, far_merid = product(
        in_hbm(conductivity), in_hbm(wind_terms), tiles, tiles.shape[0] - FAR_TILES
    )
    combined, edges = integral(
        tile_targets, level_weights, gathered, (near_plain, near_zonal), (far_plain, far_zonal)
    )
    edges, near_merid = lax.optimization_barrier((edges, near_merid))
    inside, across = lon_neighbours(edges)
    merid = meridional(tile_targets, level_weights, gathered, near_merid, far_merid)
    sends = assemble(combined, merid, inside, across)
    received = lax.all_to_all(sends, "lat", 0, 0, tiled=True)
    geo_field = backward(tile_targets, gathered, inside, across, tiles)
    stencil, source_term = stencil_source(received)
    return stencil, source_term, geo_field


def solution(mesh):
    in_specs = (
        P(None, None, ("lat", "lon")),
        P(None, None, ("lat", "lon")),
        P(("lat", "lon"), None, None),
        P(("lat", "lon"), None),
        P(),
        P(None, "lat", "lon"),
        P("lat", "lon"),
    )
    out_specs = (P(None, "lat", "lon"), P("lat", "lon"), P(None, ("lat", "lon")))
    return jax.shard_map(
        per_device, mesh=mesh, in_specs=in_specs, out_specs=out_specs, check_vma=False
    )
```

```python
import functools

import jax
import jax.numpy as jnp
from jax import lax
from jax.experimental import pallas as pl
from jax.experimental.pallas import tpu as pltpu
from jax.sharding import PartitionSpec as P

RADIX = 128.0
ROWS, COLS = 8, 128
SUM_ROWS = 64
SCOPED = 24 * 2**20
SMALL = 8 * 2**20
CHUNK = 2 * COLS
FAR_TILES = 2
ORDER = [5, 6, 9, 10, 1, 2, 4, 7, 8, 11, 13, 14, 0, 3, 12, 15]
VMEM_SPEC = pl.BlockSpec(memory_space=pltpu.VMEM)
HBM_SPEC = pl.BlockSpec(memory_space=pltpu.HBM)
SMEM_SPEC = pl.BlockSpec(memory_space=pltpu.SMEM)


def pack_kernel(levels_ref, potential_ref, out_ref):
    packed = levels_ref[0].astype(jnp.float32) * RADIX + levels_ref[1].astype(jnp.float32)
    potential = potential_ref[...]
    for target in range(out_ref.shape[0]):
        out_ref[target, 0:ROWS, :] = packed
        out_ref[target, ROWS : 2 * ROWS, :] = potential


def pack(line_levels, potential, n_lat):
    return pl.pallas_call(
        pack_kernel,
        out_shape=pltpu.VMEM((n_lat, 2 * ROWS, COLS), jnp.float32),
        in_specs=[VMEM_SPEC] * 2,
        out_specs=VMEM_SPEC,
        name="pack_levels_potential",
    )(line_levels, potential)


def row_above(block, edge):
    rows = lax.broadcasted_iota(jnp.int32, block.shape, 0)
    return jnp.where(rows == ROWS - 1, edge, pltpu.roll(block, ROWS - 1, 0))


def row_below(block, edge):
    rows = lax.broadcasted_iota(jnp.int32, block.shape, 0)
    return jnp.where(rows == 0, edge, pltpu.roll(block, 1, 0))


def in_vmem(array):
    return pltpu.with_memory_space_constraint(array, pltpu.VMEM)


def in_smem(array):
    return pltpu.with_memory_space_constraint(array, pltpu.SMEM)


def in_hbm(array):
    return pltpu.with_memory_space_constraint(array, pltpu.HBM)


def product_kernel(
    conductivity_hbm, wind_hbm, tiles_hbm, near_plain, near_zonal, near_merid, far_plain_hbm, far_zonal_hbm, far_merid_hbm,
    fields, conductivity, wind, tiles, far_plain, far_zonal, far_merid, sems, far_sems,
):
    tile_count, mag_cells, geo_cells = tiles.shape
    levels_n = conductivity.shape[1]
    near_count = near_plain.shape[0]
    order = list(range(near_count, tile_count)) + list(range(near_count))
    far_merid_count = far_merid.shape[0]
    field_copies = [
        pltpu.make_async_copy(conductivity_hbm, conductivity, sems.at[tile_count]),
        pltpu.make_async_copy(wind_hbm, wind, sems.at[tile_count + 1]),
    ]
    tile_copies = {
        k: pltpu.make_async_copy(tiles_hbm.at[k], tiles.at[k], sems.at[k]) for k in order
    }
    for copy in field_copies + [tile_copies[k] for k in order]:
        copy.start()
    for copy in field_copies:
        copy.wait()
    fields[0:levels_n, :] = conductivity[0]
    fields[levels_n : 2 * levels_n, :] = conductivity[1]
    first, second, third, fourth = (wind[i].astype(jnp.float32) for i in range(4))
    fields[2 * levels_n : 3 * levels_n, :] = (third - second).astype(jnp.bfloat16)
    fields[3 * levels_n : 4 * levels_n, :] = (first + fourth).astype(jnp.bfloat16)
    outputs = []

    def send(source, target):
        copy = pltpu.make_async_copy(source, target, far_sems.at[len(outputs)])
        copy.start()
        outputs.append(copy)

    for step, k in enumerate(order):
        tile_copies[k].wait()
        near, i = k < near_count, k if k < near_count else k - near_count
        plain_out, zonal_out = (near_plain, near_zonal) if near else (far_plain, far_zonal)
        merid_out, m = (far_merid, step) if step < far_merid_count else (near_merid, step - far_merid_count)
        for start in range(0, mag_cells, CHUNK):
            columns = slice(start, start + CHUNK)
            value = lax.dot_general(
                fields[...],
                tiles[k, columns, :],
                (((1,), (1,)), ((), ())),
                preferred_element_type=jnp.float32,
            )
            plain_out[i, :, columns] = value[: 2 * levels_n].astype(jnp.bfloat16)
            zonal_out[i, :, columns] = value[2 * levels_n : 3 * levels_n]
            merid_out[m, :, columns] = value[3 * levels_n :]
        if not near:
            send(far_plain.at[i], far_plain_hbm.at[i])
            send(far_zonal.at[i], far_zonal_hbm.at[i])
        if step < far_merid_count:
            send(far_merid.at[m], far_merid_hbm.at[m])
    for copy in outputs:
        copy.wait()


def product(conductivity, wind, tiles, near_count):
    levels_n, geo_cells = conductivity.shape[1:]
    tile_count, mag_cells = tiles.shape[:2]
    far_count = tile_count - near_count
    plain = lambda count: ((count, 2 * levels_n, mag_cells), jnp.bfloat16)
    wind_term = lambda count: ((count, levels_n, mag_cells), jnp.float32)
    return pl.pallas_call(
        product_kernel,
        out_shape=(
            pltpu.VMEM(*plain(near_count)),
            pltpu.VMEM(*wind_term(near_count)),
            pltpu.VMEM(*wind_term(1)),
            pltpu.HBM(*plain(far_count)),
            pltpu.HBM(*wind_term(far_count)),
            pltpu.HBM(*wind_term(tile_count - 1)),
        ),
        in_specs=[HBM_SPEC] * 3,
        out_specs=(VMEM_SPEC,) * 3 + (HBM_SPEC,) * 3,
        scratch_shapes=[
            pltpu.VMEM((4 * levels_n, geo_cells), jnp.bfloat16),
            pltpu.VMEM(conductivity.shape, conductivity.dtype),
            pltpu.VMEM(wind.shape, wind.dtype),
            pltpu.VMEM(tiles.shape, tiles.dtype),
            pltpu.VMEM(*plain(far_count)),
            pltpu.VMEM(*wind_term(far_count)),
            pltpu.VMEM(*wind_term(tile_count - 1)),
            pltpu.SemaphoreType.DMA((tile_count + 2,)),
            pltpu.SemaphoreType.DMA((2 * far_count + tile_count - 1,)),
        ],
        compiler_params=pltpu.CompilerParams(vmem_limit_bytes=SCOPED),
        cost_estimate=pl.CostEstimate(
            flops=2 * 4 * levels_n * tiles.size, bytes_accessed=2 * tiles.size, transcendentals=0
        ),
        name="regrid_product",
    )(conductivity, wind, tiles)


def masked_weights(target, row, gathered, weights):
    levels_n = weights.shape[0]
    level_of = lax.broadcasted_iota(jnp.int32, (levels_n, COLS), 0).astype(jnp.float32)
    bounds = gathered[target, row : row + 1, :]
    low = jnp.floor(bounds * (1.0 / RADIX))
    high = bounds - low * RADIX
    inside = (level_of >= low) & (level_of < high)
    return jnp.where(inside, weights[...], 0.0)


def fill_weights(level_weights, weights):
    for level in range(weights.shape[0]):
        weights[level : level + 1, :] = jnp.full((1, COLS), level_weights[level], jnp.float32)


def integral_kernel(
    targets, level_weights, gathered, near_plain, near_zonal, far_plain_hbm, far_zonal_hbm, combined, edges,
    weights, plain, mirrored, far_plain, far_zonal, sems,
):
    near_count, far_count = near_plain.shape[0], far_plain.shape[0]
    levels_n = level_weights.shape[0]
    n_lat = gathered.shape[0]

    def far_inputs(i):
        return (
            pltpu.make_async_copy(far_plain_hbm.at[i], far_plain.at[i], sems.at[2 * i]),
            pltpu.make_async_copy(far_zonal_hbm.at[i], far_zonal.at[i], sems.at[2 * i + 1]),
        )

    for i in range(far_count):
        for copy in far_inputs(i):
            copy.start()
    fill_weights(level_weights, weights)
    plain[...] = jnp.zeros_like(plain)
    mirrored[...] = jnp.zeros_like(mirrored)

    def integrate(k, plain_part, zonal_part, i):
        target = targets[0, k]
        opposite = n_lat - 1 - target
        for row in range(ROWS):
            columns = slice(row * COLS, (row + 1) * COLS)
            weight = masked_weights(target, row, gathered, weights)
            for f in range(3):
                planes = zonal_part if f == 2 else plain_part
                start = 0 if f == 2 else f * levels_n
                part = planes[i, start : start + levels_n, columns]
                total = jnp.sum(part.astype(jnp.float32) * weight, axis=0, keepdims=True)
                plain[target, f * ROWS + row : f * ROWS + row + 1, :] = total
                last = (f + 1) * ROWS - 1 - row
                mirrored[opposite, last : last + 1, :] = total

    @pl.loop(0, near_count)
    def _(i):
        integrate(i, near_plain, near_zonal, i)

    @pl.loop(0, far_count)
    def _(i):
        for copy in far_inputs(i):
            copy.wait()
        integrate(near_count + i, far_plain, far_zonal, i)

    lanes = lax.broadcasted_iota(jnp.int32, (ROWS, COLS), 1)
    for b in range(n_lat):
        combined[b] = plain[b] + mirrored[b]

    def both_edges(block_of):
        edge = jnp.zeros((ROWS, COLS), jnp.float32)
        for b in range(n_lat):
            block = block_of(b)
            edge = jnp.where(lanes == 2 * b, pltpu.roll(block, 2 * b, 1), edge)
            edge = jnp.where(lanes == 2 * b + 1, pltpu.roll(block, 2 * b + 2, 1), edge)
        return edge

    for f in range(3):
        rows = slice(f * ROWS, (f + 1) * ROWS)
        edges[rows, :] = both_edges(lambda b: combined[b, rows, :])
    edges[3 * ROWS : 4 * ROWS, :] = both_edges(lambda b: gathered[b, ROWS : 2 * ROWS, :])


def integral(targets, level_weights, gathered, near, far):
    far_count = far[0].shape[0]
    levels_n = level_weights.shape[0]
    n_lat = gathered.shape[0]
    return pl.pallas_call(
        integral_kernel,
        out_shape=(
            pltpu.VMEM((n_lat, 3 * ROWS, COLS), jnp.float32),
            pltpu.VMEM((4 * ROWS, COLS), jnp.float32),
        ),
        in_specs=[SMEM_SPEC] * 2 + [VMEM_SPEC] * 3 + [HBM_SPEC] * 2,
        out_specs=(VMEM_SPEC, VMEM_SPEC),
        scratch_shapes=[
            pltpu.VMEM((levels_n, COLS), jnp.float32),
            pltpu.VMEM((n_lat, 3 * ROWS, COLS), jnp.float32),
            pltpu.VMEM((n_lat, 3 * ROWS, COLS), jnp.float32),
            pltpu.VMEM(far[0].shape, far[0].dtype),
            pltpu.VMEM(far[1].shape, far[1].dtype),
            pltpu.SemaphoreType.DMA((2 * far_count,)),
        ],
        compiler_params=pltpu.CompilerParams(vmem_limit_bytes=SCOPED),
        cost_estimate=pl.CostEstimate(
            flops=6 * near[0].size, bytes_accessed=16 * near[0].size, transcendentals=0
        ),
        name="level_integral",
    )(in_smem(targets), in_smem(level_weights), in_vmem(gathered), *map(in_vmem, near), *map(in_hbm, far))


def meridional_kernel(
    targets, level_weights, gathered, near, far_hbm, out_ref, weights, total, far, sems
):
    far_count = far.shape[0]
    tile_count = targets.shape[1]
    levels_n = level_weights.shape[0]
    n_lat = gathered.shape[0]
    shift = tile_count - FAR_TILES

    def far_input(i):
        return pltpu.make_async_copy(far_hbm.at[i], far.at[i], sems.at[i])

    for i in range(far_count):
        far_input(i).start()
    fill_weights(level_weights, weights)
    total[...] = jnp.zeros_like(total)

    def integrate(step, planes, i):
        target = targets[0, lax.rem(step + shift, tile_count)]
        for row in range(ROWS):
            columns = slice(row * COLS, (row + 1) * COLS)
            weight = masked_weights(target, row, gathered, weights)
            value = jnp.sum(planes[i, :, columns] * weight, axis=0, keepdims=True)
            total[0, target, row : row + 1, :] = value
            total[1, n_lat - 1 - target, ROWS - 1 - row : ROWS - row, :] = value

    integrate(far_count, near, 0)

    @pl.loop(0, far_count)
    def _(i):
        far_input(i).wait()
        integrate(i, far, i)

    merid = [total[0, b] + total[1, b] for b in range(n_lat)]
    nothing = jnp.zeros((1, COLS), jnp.float32)
    for b in range(n_lat):
        below = merid[b - 1][ROWS - 1 : ROWS] if b > 0 else nothing
        above = merid[b + 1][0:1] if b + 1 < n_lat else nothing
        out_ref[b] = row_below(merid[b], below) - row_above(merid[b], above)


def meridional(targets, level_weights, gathered, near, far):
    n_lat = gathered.shape[0]
    levels_n = level_weights.shape[0]
    return pl.pallas_call(
        meridional_kernel,
        out_shape=pltpu.VMEM((n_lat, ROWS, COLS), jnp.float32),
        in_specs=[SMEM_SPEC] * 2 + [VMEM_SPEC] * 2 + [HBM_SPEC],
        out_specs=VMEM_SPEC,
        scratch_shapes=[
            pltpu.VMEM((levels_n, COLS), jnp.float32),
            pltpu.VMEM((2, n_lat, ROWS, COLS), jnp.float32),
            pltpu.VMEM(far.shape, far.dtype),
            pltpu.SemaphoreType.DMA((far.shape[0],)),
        ],
        compiler_params=pltpu.CompilerParams(vmem_limit_bytes=SCOPED),
        cost_estimate=pl.CostEstimate(
            flops=4 * far.size, bytes_accessed=8 * far.size, transcendentals=0
        ),
        name="meridional_integral",
    )(in_smem(targets), in_smem(level_weights), in_vmem(gathered), in_vmem(near), in_hbm(far))


def assemble_kernel(combined, merid, inside, across, out_ref):
    n_lat = combined.shape[0]
    lanes = lax.broadcasted_iota(jnp.int32, (ROWS, COLS), 1)
    beyond = []
    for f in range(3):
        rows = slice(f * ROWS, (f + 1) * ROWS)
        west, east = west_and_east(inside[rows, :], across[rows, :])
        beyond.append(jnp.where(lanes % 2 == 0, east, west))
    corners = [pltpu.roll(beyond[1], (COLS - 2 * b) % COLS, 1) for b in range(n_lat)]
    nothing = jnp.zeros((1, COLS), jnp.float32)
    for b in range(n_lat):
        def below(blocks):
            return blocks(b - 1)[ROWS - 1 : ROWS] if b > 0 else nothing

        def above(blocks):
            return blocks(b + 1)[0:1] if b + 1 < n_lat else nothing

        outside = [
            below(lambda i: combined[i, 0:8]),
            above(lambda i: combined[i, 0:8]),
            below(lambda i: combined[i, 8:16]),
            above(lambda i: combined[i, 8:16]),
            below(lambda i: corners[i]),
            above(lambda i: corners[i]),
            nothing,
            nothing,
        ]
        columns = jnp.zeros((ROWS, COLS), jnp.float32)
        for f in range(3):
            moved = pltpu.roll(beyond[f], (COLS + 2 * f - 2 * b) % COLS, 1)
            columns = jnp.where((lanes >= 2 * f) & (lanes < 2 * f + 2), moved, columns)

        def put(start, *blocks):
            out_ref[ORDER.index(b), start : start + 2 * ROWS, :] = jnp.concatenate(blocks, 0).astype(jnp.bfloat16)

        put(0, combined[b, 0:8], combined[b, 8:16])
        put(16, *both_parts(combined[b, 16:24]))
        put(32, *both_parts(merid[b]))
        put(48, *outside, columns)


def both_parts(block):
    first = block.astype(jnp.bfloat16).astype(jnp.float32)
    return first, block - first


def assemble(combined, merid, inside, across):
    return pl.pallas_call(
        assemble_kernel,
        out_shape=jax.ShapeDtypeStruct((combined.shape[0], SUM_ROWS, COLS), jnp.bfloat16),
        in_specs=[VMEM_SPEC] * 4,
        out_specs=VMEM_SPEC,
        compiler_params=pltpu.CompilerParams(vmem_limit_bytes=SMALL),
        name="assemble_sends",
    )(in_vmem(combined), in_vmem(merid), in_vmem(inside), in_vmem(across))


def backward_kernel(targets, gathered, inside, across, tiles_hbm, out_ref, zonal, merid, rows_ref, tiles, sems):
    n_lat = gathered.shape[0]
    tile_count = tiles.shape[0]
    copies = [
        pltpu.make_async_copy(tiles_hbm.at[k], tiles.at[k], sems.at[k]) for k in range(tile_count)
    ]
    for copy in copies:
        copy.start()
    lanes = lax.broadcasted_iota(jnp.int32, (ROWS, COLS), 1)
    nothing = jnp.zeros((1, COLS), jnp.float32)
    west_edges, east_edges = west_and_east(inside[3 * ROWS :, :], across[3 * ROWS :, :])
    for b in range(n_lat):
        here = gathered[b, ROWS : 2 * ROWS, :]
        shift = COLS - 1 - 2 * b
        eastern = jnp.where(
            lanes == COLS - 1, pltpu.roll(east_edges, shift, 1), pltpu.roll(here, COLS - 1, 1)
        )
        western = jnp.where(lanes == 0, pltpu.roll(west_edges, shift, 1), pltpu.roll(here, 1, 1))
        above = gathered[b + 1, ROWS : ROWS + 1, :] if b + 1 < n_lat else nothing
        below = gathered[b - 1, 2 * ROWS - 1 : 2 * ROWS, :] if b > 0 else nothing
        zonal[b] = -0.5 * (eastern - western)
        merid[b] = -0.5 * (row_above(here, above) - row_below(here, below))
    rows_ref[...] = jnp.zeros_like(rows_ref)
    for k in range(tile_count):
        target = targets[0, k]
        for row in range(ROWS):
            columns = slice(row * COLS, (row + 1) * COLS)
            rows_ref[k, 0:1, columns] = zonal[target, row : row + 1, :]
            rows_ref[k, 1:2, columns] = merid[target, row : row + 1, :]
    total = jnp.zeros((ROWS, tiles.shape[2]), jnp.float32)
    for k in range(tile_count):
        copies[k].wait()
        total += jnp.dot(
            rows_ref[k].astype(jnp.bfloat16), tiles[k], preferred_element_type=jnp.float32
        )
    out_ref[...] = total[0:2]


def backward(targets, gathered, inside, across, tiles):
    n_lat = gathered.shape[0]
    tile_count, mag_cells, geo_cells = tiles.shape
    return pl.pallas_call(
        backward_kernel,
        out_shape=jax.ShapeDtypeStruct((2, geo_cells), jnp.float32),
        in_specs=[SMEM_SPEC, VMEM_SPEC, VMEM_SPEC, VMEM_SPEC, HBM_SPEC],
        out_specs=VMEM_SPEC,
        scratch_shapes=[
            pltpu.VMEM((n_lat, ROWS, COLS), jnp.float32),
            pltpu.VMEM((n_lat, ROWS, COLS), jnp.float32),
            pltpu.VMEM((tile_count, ROWS, mag_cells), jnp.float32),
            pltpu.VMEM(tiles.shape, tiles.dtype),
            pltpu.SemaphoreType.DMA((tile_count,)),
        ],
        compiler_params=pltpu.CompilerParams(vmem_limit_bytes=SCOPED),
        cost_estimate=pl.CostEstimate(
            flops=16 * tiles.size, bytes_accessed=2 * tiles.size, transcendentals=0
        ),
        name="electric_to_geo",
    )(in_smem(targets), in_vmem(gathered), in_vmem(inside), in_vmem(across), tiles)


def stencil_kernel(received, stencil_ref, source_ref):
    sums = received[0].astype(jnp.float32)
    for source in range(1, received.shape[0]):
        sums += received[source].astype(jnp.float32)
    lanes = lax.broadcasted_iota(jnp.int32, (ROWS, COLS), 1)

    def eastward(block, beyond, lane):
        moved = pltpu.roll(beyond, COLS - 1 - lane, 1)
        return jnp.where(lanes == COLS - 1, moved, pltpu.roll(block, COLS - 1, 1))

    def westward(block, beyond, lane):
        moved = pltpu.roll(beyond, (COLS - lane) % COLS, 1)
        return jnp.where(lanes == 0, moved, pltpu.roll(block, 1, 1))

    center0, center1, zonal, zonal_left, merid, merid_left, edge, columns = (
        sums[i * ROWS : (i + 1) * ROWS] for i in range(8)
    )
    zonal, merid = zonal + zonal_left, merid + merid_left
    corner = pltpu.roll(edge, ROWS - 2, 0)
    edge_east, edge_west = eastward(edge, corner, 0), westward(edge, corner, 1)
    east1, west1 = eastward(center1, columns, 2), westward(center1, columns, 3)
    east_coef = 0.5 * (center0 + eastward(center0, columns, 0))
    west_coef = 0.5 * (center0 + westward(center0, columns, 1))
    north_coef = 0.5 * (center0 + row_above(center0, edge[1:2]))
    south_coef = 0.5 * (center0 + row_below(center0, edge[0:1]))
    ne_coef = 0.25 * (row_above(east1, edge_east[3:4]) - center1)
    nw_coef = -0.25 * (row_above(west1, edge_west[3:4]) - center1)
    se_coef = -0.25 * (row_below(east1, edge_east[2:3]) - center1)
    sw_coef = 0.25 * (row_below(west1, edge_west[2:3]) - center1)
    others = [east_coef, west_coef, north_coef, south_coef, ne_coef, nw_coef, se_coef, sw_coef]
    stencil_ref[0] = -sum(others[1:], others[0])
    for i, coef in enumerate(others):
        stencil_ref[i + 1] = coef
    source_ref[...] = (
        0.5 * (eastward(zonal, columns, 4) - westward(zonal, columns, 5)) + 0.5 * merid
    )


def stencil_source(received):
    return pl.pallas_call(
        stencil_kernel,
        out_shape=(
            jax.ShapeDtypeStruct((9, ROWS, COLS), jnp.float32),
            jax.ShapeDtypeStruct((ROWS, COLS), jnp.float32),
        ),
        in_specs=[VMEM_SPEC],
        out_specs=(VMEM_SPEC, VMEM_SPEC),
        compiler_params=pltpu.CompilerParams(vmem_limit_bytes=SMALL),
        name="stencil_source",
    )(in_vmem(received))


def lon_neighbours(block):
    count = lax.axis_size("lon")
    inside = [(i, i ^ 1) for i in range(count)]
    across = [(i, (i + 1 if i % 2 else i - 1) % count) for i in range(count)]
    return lax.ppermute(block, "lon", inside), lax.ppermute(block, "lon", across)


def west_and_east(inside, across):
    even = lax.axis_index("lon") % 2 == 0
    return jnp.where(even, across, inside), jnp.where(even, inside, across)


def per_device(
    conductivity, wind_terms, correlation_tiles, tile_targets, level_weights, line_levels, potential
):
    n_lat = lax.axis_size("lat")
    tiles = in_hbm(correlation_tiles)
    packed = pack(line_levels, potential, n_lat)
    gathered = lax.all_to_all(packed, "lat", 0, 0, tiled=True)
    near_plain, near_zonal, near_merid, far_plain, far_zonal, far_merid = product(
        in_hbm(conductivity), in_hbm(wind_terms), tiles, tiles.shape[0] - FAR_TILES
    )
    combined, edges = integral(
        tile_targets, level_weights, gathered, (near_plain, near_zonal), (far_plain, far_zonal)
    )
    edges, near_merid = lax.optimization_barrier((edges, near_merid))
    inside, across = lon_neighbours(edges)
    merid = meridional(tile_targets, level_weights, gathered, near_merid, far_merid)
    sends = assemble(combined, merid, inside, across)
    received = lax.all_to_all(sends, "lat", 0, 0, axis_index_groups=[ORDER], tiled=True)
    geo_field = backward(tile_targets, gathered, inside, across, tiles)
    stencil, source_term = stencil_source(received)
    return stencil, source_term, geo_field


def solution(mesh):
    in_specs = (
        P(None, None, ("lat", "lon")),
        P(None, None, ("lat", "lon")),
        P(("lat", "lon"), None, None),
        P(("lat", "lon"), None),
        P(),
        P(None, "lat", "lon"),
        P("lat", "lon"),
    )
    out_specs = (P(None, "lat", "lon"), P("lat", "lon"), P(None, ("lat", "lon")))
    return jax.shard_map(
        per_device, mesh=mesh, in_specs=in_specs, out_specs=out_specs, check_vma=False
    )
```

```python
import functools

import jax
import jax.numpy as jnp
from jax import lax
from jax.experimental import pallas as pl
from jax.experimental.pallas import tpu as pltpu
from jax.sharding import PartitionSpec as P

RADIX = 128.0
ROWS, COLS = 8, 128
SUM_ROWS = 64
SCOPED = 24 * 2**20
SMALL = 8 * 2**20
CHUNK = 2 * COLS
FAR_TILES = 2
ORDER = [5, 6, 9, 10, 1, 2, 4, 7, 8, 11, 13, 14, 0, 3, 12, 15]
VMEM_SPEC = pl.BlockSpec(memory_space=pltpu.VMEM)
HBM_SPEC = pl.BlockSpec(memory_space=pltpu.HBM)
SMEM_SPEC = pl.BlockSpec(memory_space=pltpu.SMEM)


def pack_kernel(levels_ref, potential_ref, out_ref):
    packed = levels_ref[0].astype(jnp.float32) * RADIX + levels_ref[1].astype(jnp.float32)
    potential = potential_ref[...]
    for target in range(out_ref.shape[0]):
        out_ref[target, 0:ROWS, :] = packed
        out_ref[target, ROWS : 2 * ROWS, :] = potential


def pack(line_levels, potential, n_lat):
    return pl.pallas_call(
        pack_kernel,
        out_shape=pltpu.VMEM((n_lat, 2 * ROWS, COLS), jnp.float32),
        in_specs=[VMEM_SPEC] * 2,
        out_specs=VMEM_SPEC,
        name="pack_levels_potential",
    )(line_levels, potential)


def row_above(block, edge):
    rows = lax.broadcasted_iota(jnp.int32, block.shape, 0)
    return jnp.where(rows == ROWS - 1, edge, pltpu.roll(block, ROWS - 1, 0))


def row_below(block, edge):
    rows = lax.broadcasted_iota(jnp.int32, block.shape, 0)
    return jnp.where(rows == 0, edge, pltpu.roll(block, 1, 0))


def in_vmem(array):
    return pltpu.with_memory_space_constraint(array, pltpu.VMEM)


def in_smem(array):
    return pltpu.with_memory_space_constraint(array, pltpu.SMEM)


def in_hbm(array):
    return pltpu.with_memory_space_constraint(array, pltpu.HBM)


def product_kernel(
    conductivity_hbm, wind_hbm, tiles_hbm, near_plain, near_zonal, near_merid, far_plain_hbm, far_zonal_hbm, far_merid_hbm,
    fields, conductivity, wind, tiles, far_plain, far_zonal, far_merid, sems, far_sems,
):
    tile_count, mag_cells, geo_cells = tiles.shape
    levels_n = conductivity.shape[1]
    near_count = near_plain.shape[0]
    order = list(range(near_count, tile_count)) + list(range(near_count))
    far_merid_count = far_merid.shape[0]
    field_copies = [
        pltpu.make_async_copy(conductivity_hbm, conductivity, sems.at[tile_count]),
        pltpu.make_async_copy(wind_hbm, wind, sems.at[tile_count + 1]),
    ]
    tile_copies = {
        k: pltpu.make_async_copy(tiles_hbm.at[k], tiles.at[k], sems.at[k]) for k in order
    }
    for copy in field_copies + [tile_copies[k] for k in order]:
        copy.start()
    for copy in field_copies:
        copy.wait()
    fields[0:levels_n, :] = conductivity[0]
    fields[levels_n : 2 * levels_n, :] = conductivity[1]
    first, second, third, fourth = (wind[i].astype(jnp.float32) for i in range(4))
    fields[2 * levels_n : 3 * levels_n, :] = (third - second).astype(jnp.bfloat16)
    fields[3 * levels_n : 4 * levels_n, :] = (first + fourth).astype(jnp.bfloat16)
    outputs = []

    def send(source, target):
        copy = pltpu.make_async_copy(source, target, far_sems.at[len(outputs)])
        copy.start()
        outputs.append(copy)

    for step, k in enumerate(order):
        tile_copies[k].wait()
        near, i = k < near_count, k if k < near_count else k - near_count
        plain_out, zonal_out = (near_plain, near_zonal) if near else (far_plain, far_zonal)
        merid_out, m = (far_merid, step) if step < far_merid_count else (near_merid, step - far_merid_count)
        for start in range(0, mag_cells, CHUNK):
            columns = slice(start, start + CHUNK)
            value = lax.dot_general(
                fields[...],
                tiles[k, columns, :],
                (((1,), (1,)), ((), ())),
                preferred_element_type=jnp.float32,
            )
            plain_out[i, :, columns] = value[: 2 * levels_n].astype(jnp.bfloat16)
            zonal_out[i, :, columns] = value[2 * levels_n : 3 * levels_n]
            merid_out[m, :, columns] = value[3 * levels_n :]
        if not near:
            send(far_plain.at[i], far_plain_hbm.at[i])
            send(far_zonal.at[i], far_zonal_hbm.at[i])
        if step < far_merid_count:
            send(far_merid.at[m], far_merid_hbm.at[m])
    for copy in outputs:
        copy.wait()


def product(conductivity, wind, tiles, near_count):
    levels_n, geo_cells = conductivity.shape[1:]
    tile_count, mag_cells = tiles.shape[:2]
    far_count = tile_count - near_count
    plain = lambda count: ((count, 2 * levels_n, mag_cells), jnp.bfloat16)
    wind_term = lambda count: ((count, levels_n, mag_cells), jnp.float32)
    return pl.pallas_call(
        product_kernel,
        out_shape=(
            pltpu.VMEM(*plain(near_count)),
            pltpu.VMEM(*wind_term(near_count)),
            pltpu.VMEM(*wind_term(1)),
            pltpu.HBM(*plain(far_count)),
            pltpu.HBM(*wind_term(far_count)),
            pltpu.HBM(*wind_term(tile_count - 1)),
        ),
        in_specs=[HBM_SPEC] * 3,
        out_specs=(VMEM_SPEC,) * 3 + (HBM_SPEC,) * 3,
        scratch_shapes=[
            pltpu.VMEM((4 * levels_n, geo_cells), jnp.bfloat16),
            pltpu.VMEM(conductivity.shape, conductivity.dtype),
            pltpu.VMEM(wind.shape, wind.dtype),
            pltpu.VMEM(tiles.shape, tiles.dtype),
            pltpu.VMEM(*plain(far_count)),
            pltpu.VMEM(*wind_term(far_count)),
            pltpu.VMEM(*wind_term(tile_count - 1)),
            pltpu.SemaphoreType.DMA((tile_count + 2,)),
            pltpu.SemaphoreType.DMA((2 * far_count + tile_count - 1,)),
        ],
        compiler_params=pltpu.CompilerParams(vmem_limit_bytes=SCOPED),
        cost_estimate=pl.CostEstimate(
            flops=2 * 4 * levels_n * tiles.size, bytes_accessed=2 * tiles.size, transcendentals=0
        ),
        name="regrid_product",
    )(conductivity, wind, tiles)


def masked_weights(target, row, gathered, weights):
    levels_n = weights.shape[0]
    level_of = lax.broadcasted_iota(jnp.int32, (levels_n, COLS), 0).astype(jnp.float32)
    bounds = gathered[target, row : row + 1, :]
    low = jnp.floor(bounds * (1.0 / RADIX))
    high = bounds - low * RADIX
    inside = (level_of >= low) & (level_of < high)
    return jnp.where(inside, weights[...], 0.0)


def fill_weights(level_weights, weights):
    for level in range(weights.shape[0]):
        weights[level : level + 1, :] = jnp.full((1, COLS), level_weights[level], jnp.float32)


def integral_kernel(
    targets, level_weights, gathered, near_plain, near_zonal, far_plain_hbm, far_zonal_hbm, far_merid_hbm, combined, edges, far_merid,
    weights, plain, mirrored, far_plain, far_zonal, sems,
):
    near_count, far_count = near_plain.shape[0], far_plain.shape[0]
    levels_n = level_weights.shape[0]
    n_lat = gathered.shape[0]

    def far_inputs(i):
        return (
            pltpu.make_async_copy(far_plain_hbm.at[i], far_plain.at[i], sems.at[2 * i]),
            pltpu.make_async_copy(far_zonal_hbm.at[i], far_zonal.at[i], sems.at[2 * i + 1]),
        )

    for i in range(far_count):
        for copy in far_inputs(i):
            copy.start()
    rest = [
        pltpu.make_async_copy(far_merid_hbm.at[i], far_merid.at[i], sems.at[2 * far_count + i])
        for i in range(far_merid.shape[0])
    ]
    for copy in rest:
        copy.start()
    fill_weights(level_weights, weights)
    plain[...] = jnp.zeros_like(plain)
    mirrored[...] = jnp.zeros_like(mirrored)

    def integrate(k, plain_part, zonal_part, i):
        target = targets[0, k]
        opposite = n_lat - 1 - target
        for row in range(ROWS):
            columns = slice(row * COLS, (row + 1) * COLS)
            weight = masked_weights(target, row, gathered, weights)
            for f in range(3):
                planes = zonal_part if f == 2 else plain_part
                start = 0 if f == 2 else f * levels_n
                part = planes[i, start : start + levels_n, columns]
                total = jnp.sum(part.astype(jnp.float32) * weight, axis=0, keepdims=True)
                plain[target, f * ROWS + row : f * ROWS + row + 1, :] = total
                last = (f + 1) * ROWS - 1 - row
                mirrored[opposite, last : last + 1, :] = total

    @pl.loop(0, near_count)
    def _(i):
        integrate(i, near_plain, near_zonal, i)

    @pl.loop(0, far_count)
    def _(i):
        for copy in far_inputs(i):
            copy.wait()
        integrate(near_count + i, far_plain, far_zonal, i)

    lanes = lax.broadcasted_iota(jnp.int32, (ROWS, COLS), 1)
    for b in range(n_lat):
        combined[b] = plain[b] + mirrored[b]

    def both_edges(block_of):
        edge = jnp.zeros((ROWS, COLS), jnp.float32)
        for b in range(n_lat):
            block = block_of(b)
            edge = jnp.where(lanes == 2 * b, pltpu.roll(block, 2 * b, 1), edge)
            edge = jnp.where(lanes == 2 * b + 1, pltpu.roll(block, 2 * b + 2, 1), edge)
        return edge

    for f in range(3):
        rows = slice(f * ROWS, (f + 1) * ROWS)
        edges[rows, :] = both_edges(lambda b: combined[b, rows, :])
    edges[3 * ROWS : 4 * ROWS, :] = both_edges(lambda b: gathered[b, ROWS : 2 * ROWS, :])
    for copy in rest:
        copy.wait()


def integral(targets, level_weights, gathered, near, far, far_merid):
    far_count = far[0].shape[0]
    levels_n = level_weights.shape[0]
    n_lat = gathered.shape[0]
    return pl.pallas_call(
        integral_kernel,
        out_shape=(
            pltpu.VMEM((n_lat, 3 * ROWS, COLS), jnp.float32),
            pltpu.VMEM((4 * ROWS, COLS), jnp.float32),
            pltpu.VMEM(far_merid.shape, far_merid.dtype),
        ),
        in_specs=[SMEM_SPEC] * 2 + [VMEM_SPEC] * 3 + [HBM_SPEC] * 3,
        out_specs=(VMEM_SPEC,) * 3,
        scratch_shapes=[
            pltpu.VMEM((levels_n, COLS), jnp.float32),
            pltpu.VMEM((n_lat, 3 * ROWS, COLS), jnp.float32),
            pltpu.VMEM((n_lat, 3 * ROWS, COLS), jnp.float32),
            pltpu.VMEM(far[0].shape, far[0].dtype),
            pltpu.VMEM(far[1].shape, far[1].dtype),
            pltpu.SemaphoreType.DMA((2 * far_count + far_merid.shape[0],)),
        ],
        compiler_params=pltpu.CompilerParams(vmem_limit_bytes=SCOPED),
        cost_estimate=pl.CostEstimate(
            flops=6 * near[0].size, bytes_accessed=16 * near[0].size, transcendentals=0
        ),
        name="level_integral",
    )(in_smem(targets), in_smem(level_weights), in_vmem(gathered), *map(in_vmem, near), *map(in_hbm, far), in_hbm(far_merid))


def meridional_kernel(
    targets, level_weights, gathered, near, far, out_ref, weights, total
):
    far_count = far.shape[0]
    tile_count = targets.shape[1]
    levels_n = level_weights.shape[0]
    n_lat = gathered.shape[0]
    shift = tile_count - FAR_TILES

    fill_weights(level_weights, weights)
    total[...] = jnp.zeros_like(total)

    def integrate(step, planes, i):
        target = targets[0, lax.rem(step + shift, tile_count)]
        for row in range(ROWS):
            columns = slice(row * COLS, (row + 1) * COLS)
            weight = masked_weights(target, row, gathered, weights)
            value = jnp.sum(planes[i, :, columns] * weight, axis=0, keepdims=True)
            total[0, target, row : row + 1, :] = value
            total[1, n_lat - 1 - target, ROWS - 1 - row : ROWS - row, :] = value

    integrate(far_count, near, 0)

    @pl.loop(0, far_count)
    def _(i):
        integrate(i, far, i)

    merid = [total[0, b] + total[1, b] for b in range(n_lat)]
    nothing = jnp.zeros((1, COLS), jnp.float32)
    for b in range(n_lat):
        below = merid[b - 1][ROWS - 1 : ROWS] if b > 0 else nothing
        above = merid[b + 1][0:1] if b + 1 < n_lat else nothing
        out_ref[b] = row_below(merid[b], below) - row_above(merid[b], above)


def meridional(targets, level_weights, gathered, near, far):
    n_lat = gathered.shape[0]
    levels_n = level_weights.shape[0]
    return pl.pallas_call(
        meridional_kernel,
        out_shape=pltpu.VMEM((n_lat, ROWS, COLS), jnp.float32),
        in_specs=[SMEM_SPEC] * 2 + [VMEM_SPEC] * 3,
        out_specs=VMEM_SPEC,
        scratch_shapes=[
            pltpu.VMEM((levels_n, COLS), jnp.float32),
            pltpu.VMEM((2, n_lat, ROWS, COLS), jnp.float32),
        ],
        compiler_params=pltpu.CompilerParams(vmem_limit_bytes=SMALL),
        cost_estimate=pl.CostEstimate(
            flops=4 * far.size, bytes_accessed=8 * far.size, transcendentals=0
        ),
        name="meridional_integral",
    )(in_smem(targets), in_smem(level_weights), in_vmem(gathered), in_vmem(near), in_vmem(far))


def assemble_kernel(combined, merid, inside, across, out_ref):
    n_lat = combined.shape[0]
    lanes = lax.broadcasted_iota(jnp.int32, (ROWS, COLS), 1)
    beyond = []
    for f in range(3):
        rows = slice(f * ROWS, (f + 1) * ROWS)
        west, east = west_and_east(inside[rows, :], across[rows, :])
        beyond.append(jnp.where(lanes % 2 == 0, east, west))
    corners = [pltpu.roll(beyond[1], (COLS - 2 * b) % COLS, 1) for b in range(n_lat)]
    nothing = jnp.zeros((1, COLS), jnp.float32)
    for b in range(n_lat):
        def below(blocks):
            return blocks(b - 1)[ROWS - 1 : ROWS] if b > 0 else nothing

        def above(blocks):
            return blocks(b + 1)[0:1] if b + 1 < n_lat else nothing

        outside = [
            below(lambda i: combined[i, 0:8]),
            above(lambda i: combined[i, 0:8]),
            below(lambda i: combined[i, 8:16]),
            above(lambda i: combined[i, 8:16]),
            below(lambda i: corners[i]),
            above(lambda i: corners[i]),
            nothing,
            nothing,
        ]
        columns = jnp.zeros((ROWS, COLS), jnp.float32)
        for f in range(3):
            moved = pltpu.roll(beyond[f], (COLS + 2 * f - 2 * b) % COLS, 1)
            columns = jnp.where((lanes >= 2 * f) & (lanes < 2 * f + 2), moved, columns)

        def put(start, *blocks):
            out_ref[ORDER.index(b), start : start + 2 * ROWS, :] = jnp.concatenate(blocks, 0).astype(jnp.bfloat16)

        put(0, combined[b, 0:8], combined[b, 8:16])
        put(16, *both_parts(combined[b, 16:24]))
        put(32, *both_parts(merid[b]))
        put(48, *outside, columns)


def both_parts(block):
    first = block.astype(jnp.bfloat16).astype(jnp.float32)
    return first, block - first


def assemble(combined, merid, inside, across):
    return pl.pallas_call(
        assemble_kernel,
        out_shape=jax.ShapeDtypeStruct((combined.shape[0], SUM_ROWS, COLS), jnp.bfloat16),
        in_specs=[VMEM_SPEC] * 4,
        out_specs=VMEM_SPEC,
        compiler_params=pltpu.CompilerParams(vmem_limit_bytes=SMALL),
        name="assemble_sends",
    )(in_vmem(combined), in_vmem(merid), in_vmem(inside), in_vmem(across))


def backward_kernel(targets, gathered, inside, across, tiles_hbm, out_ref, zonal, merid, rows_ref, tiles, sems):
    n_lat = gathered.shape[0]
    tile_count = tiles.shape[0]
    copies = [
        pltpu.make_async_copy(tiles_hbm.at[k], tiles.at[k], sems.at[k]) for k in range(tile_count)
    ]
    for copy in copies:
        copy.start()
    lanes = lax.broadcasted_iota(jnp.int32, (ROWS, COLS), 1)
    nothing = jnp.zeros((1, COLS), jnp.float32)
    west_edges, east_edges = west_and_east(inside[3 * ROWS :, :], across[3 * ROWS :, :])
    for b in range(n_lat):
        here = gathered[b, ROWS : 2 * ROWS, :]
        shift = COLS - 1 - 2 * b
        eastern = jnp.where(
            lanes == COLS - 1, pltpu.roll(east_edges, shift, 1), pltpu.roll(here, COLS - 1, 1)
        )
        western = jnp.where(lanes == 0, pltpu.roll(west_edges, shift, 1), pltpu.roll(here, 1, 1))
        above = gathered[b + 1, ROWS : ROWS + 1, :] if b + 1 < n_lat else nothing
        below = gathered[b - 1, 2 * ROWS - 1 : 2 * ROWS, :] if b > 0 else nothing
        zonal[b] = -0.5 * (eastern - western)
        merid[b] = -0.5 * (row_above(here, above) - row_below(here, below))
    rows_ref[...] = jnp.zeros_like(rows_ref)
    for k in range(tile_count):
        target = targets[0, k]
        for row in range(ROWS):
            columns = slice(row * COLS, (row + 1) * COLS)
            rows_ref[k, 0:1, columns] = zonal[target, row : row + 1, :]
            rows_ref[k, 1:2, columns] = merid[target, row : row + 1, :]
    total = jnp.zeros((ROWS, tiles.shape[2]), jnp.float32)
    for k in range(tile_count):
        copies[k].wait()
        total += jnp.dot(
            rows_ref[k].astype(jnp.bfloat16), tiles[k], preferred_element_type=jnp.float32
        )
    out_ref[...] = total[0:2]


def backward(targets, gathered, inside, across, tiles):
    n_lat = gathered.shape[0]
    tile_count, mag_cells, geo_cells = tiles.shape
    return pl.pallas_call(
        backward_kernel,
        out_shape=jax.ShapeDtypeStruct((2, geo_cells), jnp.float32),
        in_specs=[SMEM_SPEC, VMEM_SPEC, VMEM_SPEC, VMEM_SPEC, HBM_SPEC],
        out_specs=VMEM_SPEC,
        scratch_shapes=[
            pltpu.VMEM((n_lat, ROWS, COLS), jnp.float32),
            pltpu.VMEM((n_lat, ROWS, COLS), jnp.float32),
            pltpu.VMEM((tile_count, ROWS, mag_cells), jnp.float32),
            pltpu.VMEM(tiles.shape, tiles.dtype),
            pltpu.SemaphoreType.DMA((tile_count,)),
        ],
        compiler_params=pltpu.CompilerParams(vmem_limit_bytes=SCOPED),
        cost_estimate=pl.CostEstimate(
            flops=16 * tiles.size, bytes_accessed=2 * tiles.size, transcendentals=0
        ),
        name="electric_to_geo",
    )(in_smem(targets), in_vmem(gathered), in_vmem(inside), in_vmem(across), tiles)


def stencil_kernel(received, stencil_ref, source_ref):
    sums = received[0].astype(jnp.float32)
    for source in range(1, received.shape[0]):
        sums += received[source].astype(jnp.float32)
    lanes = lax.broadcasted_iota(jnp.int32, (ROWS, COLS), 1)

    def eastward(block, beyond, lane):
        moved = pltpu.roll(beyond, COLS - 1 - lane, 1)
        return jnp.where(lanes == COLS - 1, moved, pltpu.roll(block, COLS - 1, 1))

    def westward(block, beyond, lane):
        moved = pltpu.roll(beyond, (COLS - lane) % COLS, 1)
        return jnp.where(lanes == 0, moved, pltpu.roll(block, 1, 1))

    center0, center1, zonal, zonal_left, merid, merid_left, edge, columns = (
        sums[i * ROWS : (i + 1) * ROWS] for i in range(8)
    )
    zonal, merid = zonal + zonal_left, merid + merid_left
    corner = pltpu.roll(edge, ROWS - 2, 0)
    edge_east, edge_west = eastward(edge, corner, 0), westward(edge, corner, 1)
    east1, west1 = eastward(center1, columns, 2), westward(center1, columns, 3)
    east_coef = 0.5 * (center0 + eastward(center0, columns, 0))
    west_coef = 0.5 * (center0 + westward(center0, columns, 1))
    north_coef = 0.5 * (center0 + row_above(center0, edge[1:2]))
    south_coef = 0.5 * (center0 + row_below(center0, edge[0:1]))
    ne_coef = 0.25 * (row_above(east1, edge_east[3:4]) - center1)
    nw_coef = -0.25 * (row_above(west1, edge_west[3:4]) - center1)
    se_coef = -0.25 * (row_below(east1, edge_east[2:3]) - center1)
    sw_coef = 0.25 * (row_below(west1, edge_west[2:3]) - center1)
    others = [east_coef, west_coef, north_coef, south_coef, ne_coef, nw_coef, se_coef, sw_coef]
    stencil_ref[0] = -sum(others[1:], others[0])
    for i, coef in enumerate(others):
        stencil_ref[i + 1] = coef
    source_ref[...] = (
        0.5 * (eastward(zonal, columns, 4) - westward(zonal, columns, 5)) + 0.5 * merid
    )


def stencil_source(received):
    return pl.pallas_call(
        stencil_kernel,
        out_shape=(
            jax.ShapeDtypeStruct((9, ROWS, COLS), jnp.float32),
            jax.ShapeDtypeStruct((ROWS, COLS), jnp.float32),
        ),
        in_specs=[VMEM_SPEC],
        out_specs=(VMEM_SPEC, VMEM_SPEC),
        compiler_params=pltpu.CompilerParams(vmem_limit_bytes=SMALL),
        name="stencil_source",
    )(in_vmem(received))


def lon_neighbours(block):
    count = lax.axis_size("lon")
    inside = [(i, i ^ 1) for i in range(count)]
    across = [(i, (i + 1 if i % 2 else i - 1) % count) for i in range(count)]
    return lax.ppermute(block, "lon", inside), lax.ppermute(block, "lon", across)


def west_and_east(inside, across):
    even = lax.axis_index("lon") % 2 == 0
    return jnp.where(even, across, inside), jnp.where(even, inside, across)


def per_device(
    conductivity, wind_terms, correlation_tiles, tile_targets, level_weights, line_levels, potential
):
    n_lat = lax.axis_size("lat")
    tiles = in_hbm(correlation_tiles)
    packed = pack(line_levels, potential, n_lat)
    gathered = lax.all_to_all(packed, "lat", 0, 0, tiled=True)
    near_plain, near_zonal, near_merid, far_plain, far_zonal, far_merid = product(
        in_hbm(conductivity), in_hbm(wind_terms), tiles, tiles.shape[0] - FAR_TILES
    )
    combined, edges, far_merid = integral(
        tile_targets, level_weights, gathered, (near_plain, near_zonal), (far_plain, far_zonal), far_merid
    )
    edges, near_merid = lax.optimization_barrier((edges, near_merid))
    inside, across = lon_neighbours(edges)
    merid = meridional(tile_targets, level_weights, gathered, near_merid, far_merid)
    sends = assemble(combined, merid, inside, across)
    received = lax.all_to_all(sends, "lat", 0, 0, axis_index_groups=[ORDER], tiled=True)
    geo_field = backward(tile_targets, gathered, inside, across, tiles)
    stencil, source_term = stencil_source(received)
    return stencil, source_term, geo_field


def solution(mesh):
    in_specs = (
        P(None, None, ("lat", "lon")),
        P(None, None, ("lat", "lon")),
        P(("lat", "lon"), None, None),
        P(("lat", "lon"), None),
        P(),
        P(None, "lat", "lon"),
        P("lat", "lon"),
    )
    out_specs = (P(None, "lat", "lon"), P("lat", "lon"), P(None, ("lat", "lon")))
    return jax.shard_map(
        per_device, mesh=mesh, in_specs=in_specs, out_specs=out_specs, check_vma=False
    )
```

```python
import functools

import jax
import jax.numpy as jnp
from jax import lax
from jax.experimental import pallas as pl
from jax.experimental.pallas import tpu as pltpu
from jax.sharding import PartitionSpec as P

RADIX = 128.0
ROWS, COLS = 8, 128
SUM_ROWS = 64
SCOPED = 24 * 2**20
SMALL = 8 * 2**20
CHUNK = 2 * COLS
FAR_TILES = 2
HELD_TILES = 1
HELD_PARTS = 8
ORDER = [5, 6, 9, 10, 1, 2, 4, 7, 8, 11, 13, 14, 0, 3, 12, 15]
VMEM_SPEC = pl.BlockSpec(memory_space=pltpu.VMEM)
HBM_SPEC = pl.BlockSpec(memory_space=pltpu.HBM)
SMEM_SPEC = pl.BlockSpec(memory_space=pltpu.SMEM)


def pack_kernel(levels_ref, potential_ref, out_ref):
    packed = levels_ref[0].astype(jnp.float32) * RADIX + levels_ref[1].astype(jnp.float32)
    potential = potential_ref[...]
    for target in range(out_ref.shape[0]):
        out_ref[target, 0:ROWS, :] = packed
        out_ref[target, ROWS : 2 * ROWS, :] = potential


def pack(line_levels, potential, n_lat):
    return pl.pallas_call(
        pack_kernel,
        out_shape=pltpu.VMEM((n_lat, 2 * ROWS, COLS), jnp.float32),
        in_specs=[VMEM_SPEC] * 2,
        out_specs=VMEM_SPEC,
        name="pack_levels_potential",
    )(line_levels, potential)


def row_above(block, edge):
    rows = lax.broadcasted_iota(jnp.int32, block.shape, 0)
    return jnp.where(rows == ROWS - 1, edge, pltpu.roll(block, ROWS - 1, 0))


def row_below(block, edge):
    rows = lax.broadcasted_iota(jnp.int32, block.shape, 0)
    return jnp.where(rows == 0, edge, pltpu.roll(block, 1, 0))


def in_vmem(array):
    return pltpu.with_memory_space_constraint(array, pltpu.VMEM)


def in_smem(array):
    return pltpu.with_memory_space_constraint(array, pltpu.SMEM)


def in_hbm(array):
    return pltpu.with_memory_space_constraint(array, pltpu.HBM)


def product_kernel(
    conductivity_hbm, wind_hbm, tiles_hbm, near_plain, near_zonal, near_merid, far_plain_hbm, far_zonal_hbm, far_merid_hbm,
    fields, conductivity, wind, tiles, far_plain, far_zonal, far_merid, sems, far_sems,
):
    tile_count, mag_cells, geo_cells = tiles.shape
    levels_n = conductivity.shape[1]
    near_count = near_plain.shape[0]
    order = list(range(near_count, tile_count)) + list(range(near_count))
    far_merid_count = far_merid.shape[0]
    field_copies = [
        pltpu.make_async_copy(conductivity_hbm, conductivity, sems.at[tile_count]),
        pltpu.make_async_copy(wind_hbm, wind, sems.at[tile_count + 1]),
    ]
    tile_copies = {
        k: pltpu.make_async_copy(tiles_hbm.at[k], tiles.at[k], sems.at[k]) for k in order
    }
    for copy in field_copies + [tile_copies[k] for k in order]:
        copy.start()
    for copy in field_copies:
        copy.wait()
    fields[0:levels_n, :] = conductivity[0]
    fields[levels_n : 2 * levels_n, :] = conductivity[1]
    first, second, third, fourth = (wind[i].astype(jnp.float32) for i in range(4))
    fields[2 * levels_n : 3 * levels_n, :] = (third - second).astype(jnp.bfloat16)
    fields[3 * levels_n : 4 * levels_n, :] = (first + fourth).astype(jnp.bfloat16)
    outputs = []

    def send(source, target):
        copy = pltpu.make_async_copy(source, target, far_sems.at[len(outputs)])
        copy.start()
        outputs.append(copy)

    for step, k in enumerate(order):
        tile_copies[k].wait()
        near, i = k < near_count, k if k < near_count else k - near_count
        plain_out, zonal_out = (near_plain, near_zonal) if near else (far_plain, far_zonal)
        merid_out, m = (far_merid, step) if step < far_merid_count else (near_merid, step - far_merid_count)
        for start in range(0, mag_cells, CHUNK):
            columns = slice(start, start + CHUNK)
            value = lax.dot_general(
                fields[...],
                tiles[k, columns, :],
                (((1,), (1,)), ((), ())),
                preferred_element_type=jnp.float32,
            )
            plain_out[i, :, columns] = value[: 2 * levels_n].astype(jnp.bfloat16)
            zonal_out[i, :, columns] = value[2 * levels_n : 3 * levels_n]
            merid_out[m, :, columns] = value[3 * levels_n :]
        if not near:
            send(far_plain.at[i], far_plain_hbm.at[i])
            send(far_zonal.at[i], far_zonal_hbm.at[i])
        if step < far_merid_count:
            send(far_merid.at[m], far_merid_hbm.at[m])
    for copy in outputs:
        copy.wait()


def product(conductivity, wind, tiles, near_count):
    levels_n, geo_cells = conductivity.shape[1:]
    tile_count, mag_cells = tiles.shape[:2]
    far_count = tile_count - near_count
    plain = lambda count: ((count, 2 * levels_n, mag_cells), jnp.bfloat16)
    wind_term = lambda count: ((count, levels_n, mag_cells), jnp.float32)
    return pl.pallas_call(
        product_kernel,
        out_shape=(
            pltpu.VMEM(*plain(near_count)),
            pltpu.VMEM(*wind_term(near_count)),
            pltpu.VMEM(*wind_term(1)),
            pltpu.HBM(*plain(far_count)),
            pltpu.HBM(*wind_term(far_count)),
            pltpu.HBM(*wind_term(tile_count - 1)),
        ),
        in_specs=[HBM_SPEC] * 3,
        out_specs=(VMEM_SPEC,) * 3 + (HBM_SPEC,) * 3,
        scratch_shapes=[
            pltpu.VMEM((4 * levels_n, geo_cells), jnp.bfloat16),
            pltpu.VMEM(conductivity.shape, conductivity.dtype),
            pltpu.VMEM(wind.shape, wind.dtype),
            pltpu.VMEM(tiles.shape, tiles.dtype),
            pltpu.VMEM(*plain(far_count)),
            pltpu.VMEM(*wind_term(far_count)),
            pltpu.VMEM(*wind_term(tile_count - 1)),
            pltpu.SemaphoreType.DMA((tile_count + 2,)),
            pltpu.SemaphoreType.DMA((2 * far_count + tile_count - 1,)),
        ],
        compiler_params=pltpu.CompilerParams(vmem_limit_bytes=SCOPED),
        cost_estimate=pl.CostEstimate(
            flops=2 * 4 * levels_n * tiles.size, bytes_accessed=2 * tiles.size, transcendentals=0
        ),
        name="regrid_product",
    )(conductivity, wind, tiles)


def masked_weights(target, row, gathered, weights):
    levels_n = weights.shape[0]
    level_of = lax.broadcasted_iota(jnp.int32, (levels_n, COLS), 0).astype(jnp.float32)
    bounds = gathered[target, row : row + 1, :]
    low = jnp.floor(bounds * (1.0 / RADIX))
    high = bounds - low * RADIX
    inside = (level_of >= low) & (level_of < high)
    return jnp.where(inside, weights[...], 0.0)


def fill_weights(level_weights, weights):
    for level in range(weights.shape[0]):
        weights[level : level + 1, :] = jnp.full((1, COLS), level_weights[level], jnp.float32)


def integral_kernel(
    targets, level_weights, gathered, near_plain, near_zonal, far_plain_hbm, far_zonal_hbm, far_merid_hbm, combined, edges, far_merid,
    weights, plain, mirrored, far_plain, far_zonal, sems,
):
    near_count, far_count = near_plain.shape[0], far_plain.shape[0]
    levels_n = level_weights.shape[0]
    n_lat = gathered.shape[0]

    def far_inputs(i):
        return (
            pltpu.make_async_copy(far_plain_hbm.at[i], far_plain.at[i], sems.at[2 * i]),
            pltpu.make_async_copy(far_zonal_hbm.at[i], far_zonal.at[i], sems.at[2 * i + 1]),
        )

    for i in range(far_count):
        for copy in far_inputs(i):
            copy.start()
    rest = [
        pltpu.make_async_copy(far_merid_hbm.at[i], far_merid.at[i], sems.at[2 * far_count + i])
        for i in range(far_merid.shape[0])
    ]
    for copy in rest:
        copy.start()
    fill_weights(level_weights, weights)
    plain[...] = jnp.zeros_like(plain)
    mirrored[...] = jnp.zeros_like(mirrored)

    def integrate(k, plain_part, zonal_part, i):
        target = targets[0, k]
        opposite = n_lat - 1 - target
        for row in range(ROWS):
            columns = slice(row * COLS, (row + 1) * COLS)
            weight = masked_weights(target, row, gathered, weights)
            for f in range(3):
                planes = zonal_part if f == 2 else plain_part
                start = 0 if f == 2 else f * levels_n
                part = planes[i, start : start + levels_n, columns]
                total = jnp.sum(part.astype(jnp.float32) * weight, axis=0, keepdims=True)
                plain[target, f * ROWS + row : f * ROWS + row + 1, :] = total
                last = (f + 1) * ROWS - 1 - row
                mirrored[opposite, last : last + 1, :] = total

    @pl.loop(0, near_count)
    def _(i):
        integrate(i, near_plain, near_zonal, i)

    @pl.loop(0, far_count)
    def _(i):
        for copy in far_inputs(i):
            copy.wait()
        integrate(near_count + i, far_plain, far_zonal, i)

    lanes = lax.broadcasted_iota(jnp.int32, (ROWS, COLS), 1)
    for b in range(n_lat):
        combined[b] = plain[b] + mirrored[b]

    def both_edges(block_of):
        edge = jnp.zeros((ROWS, COLS), jnp.float32)
        for b in range(n_lat):
            block = block_of(b)
            edge = jnp.where(lanes == 2 * b, pltpu.roll(block, 2 * b, 1), edge)
            edge = jnp.where(lanes == 2 * b + 1, pltpu.roll(block, 2 * b + 2, 1), edge)
        return edge

    for f in range(3):
        rows = slice(f * ROWS, (f + 1) * ROWS)
        edges[rows, :] = both_edges(lambda b: combined[b, rows, :])
    edges[3 * ROWS : 4 * ROWS, :] = both_edges(lambda b: gathered[b, ROWS : 2 * ROWS, :])
    for copy in rest:
        copy.wait()


def integral(targets, level_weights, gathered, near, far, far_merid):
    far_count = far[0].shape[0]
    levels_n = level_weights.shape[0]
    n_lat = gathered.shape[0]
    return pl.pallas_call(
        integral_kernel,
        out_shape=(
            pltpu.VMEM((n_lat, 3 * ROWS, COLS), jnp.float32),
            pltpu.VMEM((4 * ROWS, COLS), jnp.float32),
            pltpu.VMEM(far_merid.shape, far_merid.dtype),
        ),
        in_specs=[SMEM_SPEC] * 2 + [VMEM_SPEC] * 3 + [HBM_SPEC] * 3,
        out_specs=(VMEM_SPEC,) * 3,
        scratch_shapes=[
            pltpu.VMEM((levels_n, COLS), jnp.float32),
            pltpu.VMEM((n_lat, 3 * ROWS, COLS), jnp.float32),
            pltpu.VMEM((n_lat, 3 * ROWS, COLS), jnp.float32),
            pltpu.VMEM(far[0].shape, far[0].dtype),
            pltpu.VMEM(far[1].shape, far[1].dtype),
            pltpu.SemaphoreType.DMA((2 * far_count + far_merid.shape[0],)),
        ],
        compiler_params=pltpu.CompilerParams(vmem_limit_bytes=SCOPED),
        cost_estimate=pl.CostEstimate(
            flops=6 * near[0].size, bytes_accessed=16 * near[0].size, transcendentals=0
        ),
        name="level_integral",
    )(in_smem(targets), in_smem(level_weights), in_vmem(gathered), *map(in_vmem, near), *map(in_hbm, far), in_hbm(far_merid))


def meridional_kernel(
    targets, level_weights, gathered, near, far, tiles_hbm, out_ref, held, weights, total, sems
):
    first = tiles_hbm.shape[0] - held.shape[0]
    part = held.shape[1] // HELD_PARTS
    hold = [
        pltpu.make_async_copy(
            tiles_hbm.at[first, pl.ds(i * part, part)], held.at[0, pl.ds(i * part, part)], sems.at[i]
        )
        for i in range(HELD_PARTS)
    ]
    for copy in hold:
        copy.start()
    far_count = far.shape[0]
    tile_count = targets.shape[1]
    levels_n = level_weights.shape[0]
    n_lat = gathered.shape[0]
    shift = tile_count - FAR_TILES

    fill_weights(level_weights, weights)
    total[...] = jnp.zeros_like(total)

    def integrate(step, planes, i):
        target = targets[0, lax.rem(step + shift, tile_count)]
        for row in range(ROWS):
            columns = slice(row * COLS, (row + 1) * COLS)
            weight = masked_weights(target, row, gathered, weights)
            value = jnp.sum(planes[i, :, columns] * weight, axis=0, keepdims=True)
            total[0, target, row : row + 1, :] = value
            total[1, n_lat - 1 - target, ROWS - 1 - row : ROWS - row, :] = value

    integrate(far_count, near, 0)

    @pl.loop(0, far_count)
    def _(i):
        integrate(i, far, i)

    merid = [total[0, b] + total[1, b] for b in range(n_lat)]
    nothing = jnp.zeros((1, COLS), jnp.float32)
    for b in range(n_lat):
        below = merid[b - 1][ROWS - 1 : ROWS] if b > 0 else nothing
        above = merid[b + 1][0:1] if b + 1 < n_lat else nothing
        out_ref[b] = row_below(merid[b], below) - row_above(merid[b], above)
    for copy in hold:
        copy.wait()


def meridional(targets, level_weights, gathered, near, far, tiles):
    n_lat = gathered.shape[0]
    levels_n = level_weights.shape[0]
    return pl.pallas_call(
        meridional_kernel,
        out_shape=(
            pltpu.VMEM((n_lat, ROWS, COLS), jnp.float32),
            pltpu.VMEM((HELD_TILES,) + tiles.shape[1:], tiles.dtype),
        ),
        in_specs=[SMEM_SPEC] * 2 + [VMEM_SPEC] * 3 + [HBM_SPEC],
        out_specs=(VMEM_SPEC, VMEM_SPEC),
        scratch_shapes=[
            pltpu.VMEM((levels_n, COLS), jnp.float32),
            pltpu.VMEM((2, n_lat, ROWS, COLS), jnp.float32),
            pltpu.SemaphoreType.DMA((HELD_PARTS,)),
        ],
        compiler_params=pltpu.CompilerParams(vmem_limit_bytes=SMALL),
        cost_estimate=pl.CostEstimate(
            flops=4 * far.size, bytes_accessed=8 * far.size, transcendentals=0
        ),
        name="meridional_integral",
    )(in_smem(targets), in_smem(level_weights), in_vmem(gathered), in_vmem(near), in_vmem(far), in_hbm(tiles))


def assemble_kernel(combined, merid, inside, across, out_ref):
    n_lat = combined.shape[0]
    lanes = lax.broadcasted_iota(jnp.int32, (ROWS, COLS), 1)
    beyond = []
    for f in range(3):
        rows = slice(f * ROWS, (f + 1) * ROWS)
        west, east = west_and_east(inside[rows, :], across[rows, :])
        beyond.append(jnp.where(lanes % 2 == 0, east, west))
    corners = [pltpu.roll(beyond[1], (COLS - 2 * b) % COLS, 1) for b in range(n_lat)]
    nothing = jnp.zeros((1, COLS), jnp.float32)
    for b in range(n_lat):
        def below(blocks):
            return blocks(b - 1)[ROWS - 1 : ROWS] if b > 0 else nothing

        def above(blocks):
            return blocks(b + 1)[0:1] if b + 1 < n_lat else nothing

        outside = [
            below(lambda i: combined[i, 0:8]),
            above(lambda i: combined[i, 0:8]),
            below(lambda i: combined[i, 8:16]),
            above(lambda i: combined[i, 8:16]),
            below(lambda i: corners[i]),
            above(lambda i: corners[i]),
            nothing,
            nothing,
        ]
        columns = jnp.zeros((ROWS, COLS), jnp.float32)
        for f in range(3):
            moved = pltpu.roll(beyond[f], (COLS + 2 * f - 2 * b) % COLS, 1)
            columns = jnp.where((lanes >= 2 * f) & (lanes < 2 * f + 2), moved, columns)

        def put(start, *blocks):
            out_ref[ORDER.index(b), start : start + 2 * ROWS, :] = jnp.concatenate(blocks, 0).astype(jnp.bfloat16)

        put(0, combined[b, 0:8], combined[b, 8:16])
        put(16, *both_parts(combined[b, 16:24]))
        put(32, *both_parts(merid[b]))
        put(48, *outside, columns)


def both_parts(block):
    first = block.astype(jnp.bfloat16).astype(jnp.float32)
    return first, block - first


def assemble(combined, merid, inside, across):
    return pl.pallas_call(
        assemble_kernel,
        out_shape=jax.ShapeDtypeStruct((combined.shape[0], SUM_ROWS, COLS), jnp.bfloat16),
        in_specs=[VMEM_SPEC] * 4,
        out_specs=VMEM_SPEC,
        compiler_params=pltpu.CompilerParams(vmem_limit_bytes=SMALL),
        name="assemble_sends",
    )(in_vmem(combined), in_vmem(merid), in_vmem(inside), in_vmem(across))


def backward_kernel(targets, gathered, inside, across, held, tiles_hbm, out_ref, zonal, merid, rows_ref, tiles, sems):
    n_lat = gathered.shape[0]
    tile_count = tiles.shape[0]
    copies = [
        pltpu.make_async_copy(tiles_hbm.at[k], tiles.at[k], sems.at[k]) for k in range(tile_count)
    ]
    for copy in copies:
        copy.start()
    lanes = lax.broadcasted_iota(jnp.int32, (ROWS, COLS), 1)
    nothing = jnp.zeros((1, COLS), jnp.float32)
    west_edges, east_edges = west_and_east(inside[3 * ROWS :, :], across[3 * ROWS :, :])
    for b in range(n_lat):
        here = gathered[b, ROWS : 2 * ROWS, :]
        shift = COLS - 1 - 2 * b
        eastern = jnp.where(
            lanes == COLS - 1, pltpu.roll(east_edges, shift, 1), pltpu.roll(here, COLS - 1, 1)
        )
        western = jnp.where(lanes == 0, pltpu.roll(west_edges, shift, 1), pltpu.roll(here, 1, 1))
        above = gathered[b + 1, ROWS : ROWS + 1, :] if b + 1 < n_lat else nothing
        below = gathered[b - 1, 2 * ROWS - 1 : 2 * ROWS, :] if b > 0 else nothing
        zonal[b] = -0.5 * (eastern - western)
        merid[b] = -0.5 * (row_above(here, above) - row_below(here, below))
    rows_ref[...] = jnp.zeros_like(rows_ref)
    for k in range(rows_ref.shape[0]):
        target = targets[0, k]
        for row in range(ROWS):
            columns = slice(row * COLS, (row + 1) * COLS)
            rows_ref[k, 0:1, columns] = zonal[target, row : row + 1, :]
            rows_ref[k, 1:2, columns] = merid[target, row : row + 1, :]
    total = jnp.zeros((ROWS, tiles.shape[2]), jnp.float32)
    for i in range(held.shape[0]):
        total += jnp.dot(
            rows_ref[tile_count + i].astype(jnp.bfloat16), held[i], preferred_element_type=jnp.float32
        )
    for k in range(tile_count):
        copies[k].wait()
        total += jnp.dot(
            rows_ref[k].astype(jnp.bfloat16), tiles[k], preferred_element_type=jnp.float32
        )
    out_ref[...] = total[0:2]


def backward(targets, gathered, inside, across, held, tiles):
    n_lat = gathered.shape[0]
    tile_count, mag_cells, geo_cells = tiles.shape
    return pl.pallas_call(
        backward_kernel,
        out_shape=jax.ShapeDtypeStruct((2, geo_cells), jnp.float32),
        in_specs=[SMEM_SPEC] + [VMEM_SPEC] * 4 + [HBM_SPEC],
        out_specs=VMEM_SPEC,
        scratch_shapes=[
            pltpu.VMEM((n_lat, ROWS, COLS), jnp.float32),
            pltpu.VMEM((n_lat, ROWS, COLS), jnp.float32),
            pltpu.VMEM((tile_count, ROWS, mag_cells), jnp.float32),
            pltpu.VMEM((tile_count - held.shape[0], mag_cells, geo_cells), tiles.dtype),
            pltpu.SemaphoreType.DMA((tile_count - held.shape[0],)),
        ],
        compiler_params=pltpu.CompilerParams(vmem_limit_bytes=SCOPED),
        cost_estimate=pl.CostEstimate(
            flops=16 * tiles.size, bytes_accessed=2 * tiles.size, transcendentals=0
        ),
        name="electric_to_geo",
    )(in_smem(targets), in_vmem(gathered), in_vmem(inside), in_vmem(across), in_vmem(held), tiles)


def stencil_kernel(received, stencil_ref, source_ref):
    sums = received[0].astype(jnp.float32)
    for source in range(1, received.shape[0]):
        sums += received[source].astype(jnp.float32)
    lanes = lax.broadcasted_iota(jnp.int32, (ROWS, COLS), 1)

    def eastward(block, beyond, lane):
        moved = pltpu.roll(beyond, COLS - 1 - lane, 1)
        return jnp.where(lanes == COLS - 1, moved, pltpu.roll(block, COLS - 1, 1))

    def westward(block, beyond, lane):
        moved = pltpu.roll(beyond, (COLS - lane) % COLS, 1)
        return jnp.where(lanes == 0, moved, pltpu.roll(block, 1, 1))

    center0, center1, zonal, zonal_left, merid, merid_left, edge, columns = (
        sums[i * ROWS : (i + 1) * ROWS] for i in range(8)
    )
    zonal, merid = zonal + zonal_left, merid + merid_left
    corner = pltpu.roll(edge, ROWS - 2, 0)
    edge_east, edge_west = eastward(edge, corner, 0), westward(edge, corner, 1)
    east1, west1 = eastward(center1, columns, 2), westward(center1, columns, 3)
    east_coef = 0.5 * (center0 + eastward(center0, columns, 0))
    west_coef = 0.5 * (center0 + westward(center0, columns, 1))
    north_coef = 0.5 * (center0 + row_above(center0, edge[1:2]))
    south_coef = 0.5 * (center0 + row_below(center0, edge[0:1]))
    ne_coef = 0.25 * (row_above(east1, edge_east[3:4]) - center1)
    nw_coef = -0.25 * (row_above(west1, edge_west[3:4]) - center1)
    se_coef = -0.25 * (row_below(east1, edge_east[2:3]) - center1)
    sw_coef = 0.25 * (row_below(west1, edge_west[2:3]) - center1)
    others = [east_coef, west_coef, north_coef, south_coef, ne_coef, nw_coef, se_coef, sw_coef]
    stencil_ref[0] = -sum(others[1:], others[0])
    for i, coef in enumerate(others):
        stencil_ref[i + 1] = coef
    source_ref[...] = (
        0.5 * (eastward(zonal, columns, 4) - westward(zonal, columns, 5)) + 0.5 * merid
    )


def stencil_source(received):
    return pl.pallas_call(
        stencil_kernel,
        out_shape=(
            jax.ShapeDtypeStruct((9, ROWS, COLS), jnp.float32),
            jax.ShapeDtypeStruct((ROWS, COLS), jnp.float32),
        ),
        in_specs=[VMEM_SPEC],
        out_specs=(VMEM_SPEC, VMEM_SPEC),
        compiler_params=pltpu.CompilerParams(vmem_limit_bytes=SMALL),
        name="stencil_source",
    )(in_vmem(received))


def lon_neighbours(block):
    count = lax.axis_size("lon")
    inside = [(i, i ^ 1) for i in range(count)]
    across = [(i, (i + 1 if i % 2 else i - 1) % count) for i in range(count)]
    return lax.ppermute(block, "lon", inside), lax.ppermute(block, "lon", across)


def west_and_east(inside, across):
    even = lax.axis_index("lon") % 2 == 0
    return jnp.where(even, across, inside), jnp.where(even, inside, across)


def per_device(
    conductivity, wind_terms, correlation_tiles, tile_targets, level_weights, line_levels, potential
):
    n_lat = lax.axis_size("lat")
    tiles = in_hbm(correlation_tiles)
    packed = pack(line_levels, potential, n_lat)
    gathered = lax.all_to_all(packed, "lat", 0, 0, tiled=True)
    near_plain, near_zonal, near_merid, far_plain, far_zonal, far_merid = product(
        in_hbm(conductivity), in_hbm(wind_terms), tiles, tiles.shape[0] - FAR_TILES
    )
    combined, edges, far_merid = integral(
        tile_targets, level_weights, gathered, (near_plain, near_zonal), (far_plain, far_zonal), far_merid
    )
    edges, near_merid = lax.optimization_barrier((edges, near_merid))
    inside, across = lon_neighbours(edges)
    merid, held = meridional(
        tile_targets, level_weights, gathered, near_merid, far_merid, tiles
    )
    sends = assemble(combined, merid, inside, across)
    received = lax.all_to_all(sends, "lat", 0, 0, axis_index_groups=[ORDER], tiled=True)
    geo_field = backward(tile_targets, gathered, inside, across, held, tiles)
    stencil, source_term = stencil_source(received)
    return stencil, source_term, geo_field


def solution(mesh):
    in_specs = (
        P(None, None, ("lat", "lon")),
        P(None, None, ("lat", "lon")),
        P(("lat", "lon"), None, None),
        P(("lat", "lon"), None),
        P(),
        P(None, "lat", "lon"),
        P("lat", "lon"),
    )
    out_specs = (P(None, "lat", "lon"), P("lat", "lon"), P(None, ("lat", "lon")))
    return jax.shard_map(
        per_device, mesh=mesh, in_specs=in_specs, out_specs=out_specs, check_vma=False
    )
```
